256 devices in a mesh: role: 64 (over x, y, z_hi, core), tp: 4 (over z_lo).
Axes of the slice: x: 4, y: 4, z: 8 (z_hi: 2, z_lo: 4; z = z_hi * 4 + z_lo), core: 2. Of those that a mesh axis runs over, the one named last changes fastest.
Arguments:
- prompt_q: bfloat16 [64, 64, 8192], P('role', None, 'tp'), may hold values from -60 to 60
- prompt_kv: bfloat16 [64, 2, 192, 1024], P('role', None, None, 'tp'), may hold values from -4.2 to 4.2
- prefix_length: int32 [64], P('role'), may hold values from 1 to 128
- decode_q: bfloat16 [64, 128, 2, 8192], P('role', 'tp'), may hold values from -60 to 60
- decode_kv: bfloat16 [64, 128, 2, 16, 1024], P('role', 'tp'), may hold values from -9 to 9
- fresh_kv: bfloat16 [64, 128, 2, 2, 1024], P('role', 'tp'), may hold values from -16 to 16
- source_prompt: int32 [64, 128, 1], P('role', 'tp'), may hold values from 0 to 63; in each aligned block of 32 rows (0 to 31, 32 to 63, ..., all dimensions but the last counted through in order) at most 2 rows name the same one
- cache_length: int32 [64, 128], P('role', 'tp'), may hold values from 2 to 16
Outputs:
- prompt_out: bfloat16 [64, 64, 8192], P('role', None, 'tp')
- decode_out: bfloat16 [64, 128, 2, 8192], P('role', 'tp')
The draws below stay inside these ranges and needn't reach their ends.
Inputs may be any that keep to these rules, and one draw needn't show every extreme that they name: `source_prompt`: among the 32 sequences of one device, no prompt is named more than 2 times.
All inputs are finite; a program needn't handle non-finite values.
Results may differ from the reference program's by a relative error of at most 0.0045.
Values may be sent and summed in bfloat16 or wider, within the bound.
A program may use at most 128 MiB of HBM per device.

```python
import math
import jax
import jax.numpy as jnp
import numpy as np
from jax import lax

HEADS = 64
KVH = 8
HD = 128
C = 64
PRE = 128
LOC = 16
SEQ_DEV = 32
STEPS = 2
GROUPS = 64
SEQS = 128
CAP = 2


def draw_prompt_kv(key, part):
    inner_key = jax.random.fold_in(key, 7)
    array_shape = (GROUPS, 2, PRE + C, KVH * HD)
    values_base = jnp.clip(0.7 * jax.random.normal(inner_key, array_shape, jnp.float32), -4.2, 4.2)
    return values_base.astype(jnp.bfloat16)


def draw_prompt_q(key, part):
    inner_key = jax.random.fold_in(key, 8)
    array_shape = (GROUPS, C, HEADS * HD)
    values_base = jnp.clip(jax.random.normal(inner_key, array_shape, jnp.float32), -6.0, 6.0)
    return values_base.astype(jnp.bfloat16)


def draw_decode_kv(key, part):
    inner_key = jax.random.fold_in(key, 9)
    array_shape = (GROUPS, SEQS, 2, LOC, KVH * HD)
    values_base = jnp.clip(1.5 * jax.random.normal(inner_key, array_shape, jnp.float32), -9.0, 9.0)
    return values_base.astype(jnp.bfloat16)


def draw_decode_q(key, part):
    inner_key = jax.random.fold_in(key, 10)
    array_shape = (GROUPS, SEQS, STEPS, HEADS * HD)
    values_base = jnp.clip(jax.random.normal(inner_key, array_shape, jnp.float32), -6.0, 6.0)
    return values_base.astype(jnp.bfloat16)


def draw_prefix_length(key, part):
    key = jax.random.fold_in(key, 3)
    first_key, second_key, third_key = jax.random.split(key, 3)
    halvings = jax.random.randint(first_key, (GROUPS,), 0, 4)
    shortfall = jax.random.randint(second_key, (GROUPS,), 0, PRE // 16)
    lengths = jnp.right_shift(jnp.full((GROUPS,), PRE, jnp.int32), halvings.astype(jnp.int32)) - shortfall.astype(jnp.int32)
    longest = jax.random.randint(third_key, (), 0, GROUPS)
    lengths = jnp.where(jnp.arange(GROUPS) == longest, PRE, lengths)
    return lengths.astype(jnp.int32)


def with_ends(values, own_key, least, top_value):
    index_at = [jax.random.randint(jax.random.fold_in(own_key, axis), (), 0, length) for axis, length in enumerate(values.shape)]
    widest = values.shape.index(max(values.shape))
    next_to = index_at[:widest] + [(index_at[widest] + 1) % values.shape[widest]] + index_at[widest + 1:]
    return values.at[tuple(index_at)].set(least).at[tuple(next_to)].set(top_value)


def levels(own_key, extent, shards, least, high):
    loudness, own = 1.0, jax.random.fold_in(own_key, 6)
    for dim, parts in shards:
        heights = jnp.exp(jax.random.uniform(jax.random.fold_in(own, dim), (parts,), jnp.float32, least / len(shards), high / len(shards)))
        loudness = loudness * jnp.repeat(heights, extent[dim] // parts).reshape([-1 if axis == dim else 1 for axis in range(len(extent))])
    return loudness


def routed_block(stream_key, own, number, rows, number_of, top, reach, slope):
    ranking = jax.random.permutation(stream_key, number_of)
    packed, ordinary = portions_of(number_of, rows * top, reach, slope, True), portions_of(number_of, rows * top, reach, slope, False)
    places = jnp.arange(number_of)

    def named(tallies, rotation):
        used = int((tallies > 0).sum())
        fixed = max(1, used // 4)
        moved = fixed + (places - fixed + rotation * (used - fixed)) % max(1, number_of - fixed)
        return jnp.zeros((number_of,), jnp.int32).at[ranking[jnp.where(places < fixed, places, moved)]].set(jnp.asarray(tallies, jnp.int32))

    tallies = jnp.where(number % 4 == 0, named(packed, number // 4), named(ordinary, number - number // 4 - 1))
    mixed = jax.random.permutation(jax.random.fold_in(own, 3), number_of)
    source_of, sink = mixed[0:number_of // 2 * 2:2], mixed[1:number_of // 2 * 2:2]
    slack = jnp.minimum(tallies[source_of] - 1, reach - tallies[sink]) // 2
    slack = jnp.where((source_of == ranking[0]) | (sink == ranking[0]) | (tallies[sink] == 0), 0, jnp.maximum(slack, 0))
    moved = jax.random.randint(jax.random.fold_in(own, 4), (number_of // 2,), 0, 1 << 20) % (slack + 1)
    tallies = tallies.at[source_of].add(-moved).at[sink].add(moved)
    members = jnp.searchsorted(jnp.cumsum(tallies), jnp.arange(rows * top), side="right").astype(jnp.int32)
    listing = members.reshape(top, rows).T
    listing = listing[jax.random.permutation(jax.random.fold_in(own, 1), rows)]
    rotation = jax.random.randint(jax.random.fold_in(own, 2), (rows, 1), 0, top)
    return jnp.take_along_axis(listing, (jnp.arange(top)[None, :] + rotation) % top, axis=1)


def portions_of(number_of, total, bound, lean, full):
    weights = [(1 << 20) // math.isqrt(standing ** lean) + 1 for standing in range(1, number_of + 1)]
    largest = bound if full else min(bound, max(-(-total // number_of), total * weights[0] // sum(weights)))
    least = 1 if total - largest >= number_of - 1 else 0
    counts, spare = [largest] + [least] * (number_of - 1), total - largest - least * (number_of - 1)
    while spare > 0:
        free = [i for i in range(1, number_of) if counts[i] < largest] or [i for i in range(1, number_of) if counts[i] < bound]
        whole, remaining = sum([weights[i] for i in free]), spare
        for i in free:
            addition = min(bound - counts[i], max(1, remaining * weights[i] // whole), spare)
            counts[i] = counts[i] + addition
            spare = spare - addition
    return np.array(counts)


def noise(key, dims, spread, bound, cuts=(), kind=jnp.bfloat16):
    gain = levels(key, dims, cuts, -0.22, 0.18) if cuts else 1.0
    array = jax.random.normal(key, dims, jnp.float32) * spread * gain
    return jnp.minimum(jnp.maximum(array, -bound), bound).astype(kind)


def setup_inputs(seed: int = 0) -> dict:
    arg_keys = jax.random.split(jax.random.key(seed), 9)
    prompt_q = draw_prompt_q(jax.random.fold_in(arg_keys[8], 71), 0)
    prompt_kv = draw_prompt_kv(jax.random.fold_in(arg_keys[8], 71), 0)
    prefix_length = draw_prefix_length(jax.random.fold_in(arg_keys[8], 71), 0)
    decode_q = draw_decode_q(jax.random.fold_in(arg_keys[8], 71), 0)
    decode_kv = draw_decode_kv(jax.random.fold_in(arg_keys[8], 71), 0)
    fresh_kv = noise(arg_keys[5], (GROUPS, SEQS, 2, STEPS, KVH * HD), 3.0, 16.0, ((0, 64), (1, 4)))
    source_prompt_keys = jax.random.split(jax.random.fold_in(arg_keys[6], 1), GROUPS * SEQS // SEQ_DEV)
    source_prompt_turns = jax.random.permutation(jax.random.fold_in(arg_keys[6], 3), GROUPS * SEQS // SEQ_DEV)
    source_prompt = jax.vmap(lambda own, number: routed_block(jax.random.fold_in(arg_keys[6], 2), own, number, SEQ_DEV, GROUPS, 1, CAP, 2))(source_prompt_keys, source_prompt_turns).reshape((GROUPS, SEQS, 1))
    cache_length = with_ends(jax.random.randint(arg_keys[7], (GROUPS, SEQS), 2, LOC + 1), jax.random.fold_in(arg_keys[7], 1), 2, LOC).astype(jnp.int32)
    return dict(prompt_q=prompt_q, prompt_kv=prompt_kv, prefix_length=prefix_length, decode_q=decode_q, decode_kv=decode_kv, fresh_kv=fresh_kv, source_prompt=source_prompt, cache_length=cache_length)


NEGATIVE = -1e+30

def softmax_terms(scores, usable):
    masked = jnp.where(usable, scores, NEGATIVE)
    highest = lax.optimization_barrier(jnp.max(masked, axis=-1))
    terms = jnp.where(usable, jnp.exp(masked - highest[..., None]), 0.0)
    return (highest, lax.optimization_barrier(jnp.sum(terms, axis=-1)), terms.astype(jnp.bfloat16))

def reference(prompt_q, prompt_kv, prefix_length, decode_q, decode_kv, fresh_kv, source_prompt, cache_length):
    score_scale = 1.0 / math.sqrt(HD)
    per_kv = HEADS // KVH
    key_rows = PRE + C
    positions = jnp.arange(key_rows, dtype=jnp.int32)

    def prefill(operands):
        queries, stored, prefix_rows = operands
        query_full = queries.reshape(C, KVH, per_kv, HD).astype(jnp.float32)
        key_full = stored[0].reshape(key_rows, KVH, HD).astype(jnp.float32)
        value_full = stored[1].reshape(key_rows, KVH, HD).astype(jnp.float32)
        scores = jnp.einsum('icgd,tcd->icgt', query_full, key_full) * score_scale
        own_row = jnp.arange(C, dtype=jnp.int32)[:, None]
        usable = (positions[None, :] < prefix_rows) | (positions[None, :] >= PRE) & (positions[None, :] - PRE <= own_row)
        highest, weight_sum, weights = softmax_terms(scores, usable[:, None, None, :])
        weighted = jnp.einsum('icgt,tcd->icgd', weights.astype(jnp.float32), value_full)
        return (weighted / weight_sum[..., None]).astype(jnp.bfloat16).reshape(C, HEADS * HD)
    prompt_out = lax.map(prefill, (prompt_q, prompt_kv, prefix_length))
    batch = 4
    local_rows = LOC + STEPS
    local_positions = jnp.arange(local_rows, dtype=jnp.int32)
    step_index = jnp.arange(STEPS, dtype=jnp.int32)

    def decode(operands):
        queries, cached, fresh_rows, sources, lengths = operands
        query_full = queries.reshape(batch, STEPS, KVH, per_kv, HD).astype(jnp.float32)
        chosen = prompt_kv[sources]
        key_full = chosen[:, 0].reshape(batch, key_rows, KVH, HD).astype(jnp.float32)
        value_full = chosen[:, 1].reshape(batch, key_rows, KVH, HD).astype(jnp.float32)
        scores = jnp.einsum('bscgd,btcd->bscgt', query_full, key_full) * score_scale
        prefix_rows = prefix_length[sources]
        usable = (positions[None, :] < prefix_rows[:, None]) | (positions[None, :] >= PRE)
        remote_max, remote_sum, remote_weights = softmax_terms(scores, usable[:, None, None, None, :])
        remote_out = jnp.einsum('bscgt,btcd->bscgd', remote_weights.astype(jnp.float32), value_full) / remote_sum[..., None]
        local_keys = jnp.concatenate([cached[:, 0], fresh_rows[:, 0]], axis=1).reshape(batch, local_rows, KVH, HD).astype(jnp.float32)
        local_values = jnp.concatenate([cached[:, 1], fresh_rows[:, 1]], axis=1).reshape(batch, local_rows, KVH, HD).astype(jnp.float32)
        local_scores = jnp.einsum('bscgd,btcd->bscgt', query_full, local_keys) * score_scale
        local_usable = (local_positions[None, None, :] < lengths[:, None, None]) | (local_positions[None, None, :] >= LOC) & (local_positions[None, None, :] - LOC <= step_index[None, :, None])
        local_max, local_sum, local_weights = softmax_terms(local_scores, local_usable[:, :, None, None, :])
        local_out = jnp.einsum('bscgt,btcd->bscgd', local_weights.astype(jnp.float32), local_values) / local_sum[..., None]
        joint_peak = jnp.maximum(remote_max, local_max)
        remote_share = remote_sum * jnp.exp(remote_max - joint_peak)
        local_share = local_sum * jnp.exp(local_max - joint_peak)
        merged = (remote_share[..., None] * remote_out + local_share[..., None] * local_out) / (remote_share + local_share)[..., None]
        return merged.astype(jnp.bfloat16).reshape(batch, STEPS, HEADS * HD)
    decode_out = lax.map(decode, (decode_q.reshape(-1, batch, STEPS, HEADS * HD), decode_kv.reshape(-1, batch, 2, LOC, KVH * HD), fresh_kv.reshape(-1, batch, 2, STEPS, KVH * HD), source_prompt.reshape(-1, batch), cache_length.reshape(-1, batch)))
    return (prompt_out, decode_out.reshape(GROUPS, SEQS, STEPS, HEADS * HD))
```

```python
import functools
import math

import jax
import jax.numpy as jnp
from jax import lax
from jax.experimental import pallas as pl
from jax.experimental.pallas import tpu as pltpu
from jax.sharding import PartitionSpec as P

HEADS = 64
KVH = 8
PER_KV = HEADS // KVH
HD = 128
C = 64
PRE = 128
KEYS = PRE + C
LOC = 16
SEQ = 32
STEPS = 2
ROWS = PER_KV * STEPS
NX, NY, NZH, NC, NZL = 4, 4, 2, 2, 4
RING = NZH * NZL
SLOTS = NC * NX * NY
SCALE = 1.0 / math.sqrt(HD)
NEGATIVE = -1e30
LOCAL_KEYS = KVH * (LOC + STEPS)

F32 = jnp.float32
BF16 = jnp.bfloat16
VMEM = pltpu.VMEM
MIB = 1024 * 1024


def position():
    role = lax.axis_index("role")
    z_lo = lax.axis_index("tp")
    core = lax.rem(role, NC)
    z_hi = lax.rem(role // NC, NZH)
    y = lax.rem(role // (NC * NZH), NY)
    x = role // (NC * NZH * NY)
    return x, y, z_hi, core, z_lo


def device(x, y, z_hi, core, z_lo):
    return (((x * NY + y) * NZH + z_hi) * NC + core, z_lo)


def ring_device(x, y, core, ring):
    return device(x, y, ring // NZL, core, lax.rem(ring, NZL))


def ring_head(ring):
    return 2 * lax.rem(ring, NZL) + ring // NZL


def slot_of(x, y, core):
    return (core * NX + x) * NY + y


def nt_dot(a, b):
    return lax.dot_general(a, b, (((1,), (1,)), ((), ())), preferred_element_type=F32)


def dot(a, b):
    return jnp.dot(a, b, preferred_element_type=F32)


def enter(peers):
    barrier = pltpu.get_barrier_semaphore()
    for peer in peers:
        pl.semaphore_signal(barrier, inc=1, device_id=peer, device_id_type=pl.DeviceIdType.MESH)
    pl.semaphore_wait(barrier, len(peers))


def remote(src, dst, send, recv, peer):
    return pltpu.make_async_remote_copy(
        src_ref=src,
        dst_ref=dst,
        send_sem=send,
        recv_sem=recv,
        device_id=peer,
        device_id_type=pl.DeviceIdType.MESH,
    )


def gather_kernel(
    plen, kv, q, src, ka, kb, qg, srcg, blk_a, blk_b, local, far, send_q, recv_q, send_s, recv_s,
    send_1, recv_1, send_2, recv_2, send_c, recv_c, send_f,
):
    x, y, zh, core, zl = position()
    ring = zh * NZL + zl
    sibling = device(x, y, zh, 1 - core, zl)
    ring_peers = [ring_device(x, y, core, lax.rem(ring + d, RING)) for d in range(1, RING)]
    x_peers = [device(lax.rem(x + d, NX), y, zh, core, zl) for d in range(1, NX)]
    y_peers = [device(x, lax.rem(y + d, NY), zh, core, zl) for d in range(1, NY)]

    row_bias = jnp.where(
        lax.broadcasted_iota(jnp.int32, (16, PRE), 1) < plen[0], 0.0, NEGATIVE
    ).astype(BF16)
    for half in range(2):
        columns = slice(half * HD, (half + 1) * HD)
        blk_a[half] = kv[0, 0, :, columns]
        blk_b[half, 0:KEYS] = kv[0, 1, :, columns]
        blk_b[half, KEYS:] = row_bias

    enter(ring_peers + x_peers + y_peers + [sibling])

    mine = slot_of(x, y, core)
    antipode = ring_peers[RING // 2 - 1]
    far_copies = [
        remote(blk.at[1 - zh], dst.at[mine, zh], send_f.at[i], far.at[i], antipode)
        for i, (blk, dst) in enumerate(((blk_a, ka), (blk_b, kb)))
    ]
    for copy in far_copies:
        copy.start()
    local_copies = [
        pltpu.make_async_copy(blk_a.at[zh], ka.at[mine, zh], local.at[0]),
        pltpu.make_async_copy(blk_b.at[zh], kb.at[mine, zh], local.at[1]),
        pltpu.make_async_copy(q.at[:, ring_head(ring)], qg.at[ring], local.at[2]),
        pltpu.make_async_copy(src, srcg.at[ring], local.at[3]),
    ]
    for copy in local_copies:
        copy.start()
    q_copies = []
    for d in range(1, RING):
        other = lax.rem(ring + d, RING)
        q_copies.append(
            remote(src, srcg.at[ring], send_s.at[d - 1], recv_s.at[d - 1], ring_peers[d - 1])
        )
        q_copies.append(
            remote(
                q.at[:, ring_head(other)],
                qg.at[ring],
                send_q.at[d - 1],
                recv_q.at[d - 1],
                ring_peers[d - 1],
            )
        )
    for copy in q_copies:
        copy.start()

    local_copies[0].wait()
    local_copies[1].wait()
    for copy in far_copies:
        copy.wait_recv()

    paths = ((ka, x_peers, y_peers), (kb, y_peers, x_peers))

    def slot_at(path, first, second):
        if path == 0:
            return slot_of(lax.rem(x + NX - first, NX), lax.rem(y + NY - second, NY), core)
        return slot_of(lax.rem(x + NX - second, NX), lax.rem(y + NY - first, NY), core)

    sent = []

    def push(ref, slot, send, recv, peer):
        copy = remote(ref.at[slot], ref.at[slot], send, recv, peer)
        copy.start()
        sent.append(copy)

    firsts = [[], []]
    seconds = [[], []]
    sides = []
    for path, (ref, first_peers, second_peers) in enumerate(paths):
        for d in range(1, 4):
            push(ref, mine, send_1.at[path, d - 1], recv_1.at[path, d - 1], first_peers[d - 1])
            firsts[path].append(sent[-1])
    for d in range(4):
        for path, (ref, first_peers, second_peers) in enumerate(paths):
            if d > 0:
                firsts[path][d - 1].wait_recv()
            slot = slot_at(path, d, 0)
            for e in range(1, 4):
                push(
                    ref, slot, send_2.at[path, d, e - 1], recv_2.at[path, d, e - 1],
                    second_peers[e - 1],
                )
                seconds[path].append(sent[-1])
            push(ref, slot, send_c.at[path, d, 0], recv_c.at[path, d, 0], sibling)
            sides.append(sent[-1])
    for d in range(4):
        for path, (ref, first_peers, second_peers) in enumerate(paths):
            for e in range(1, 4):
                seconds[path][d * 3 + e - 1].wait_recv()
                push(
                    ref, slot_at(path, d, e), send_c.at[path, d, e], recv_c.at[path, d, e], sibling
                )
                sides.append(sent[-1])
    for copy in sides:
        copy.wait_recv()
    for copy in q_copies:
        copy.wait()
    local_copies[2].wait()
    local_copies[3].wait()
    for copy in far_copies:
        copy.wait_send()
    for copy in sent:
        copy.wait_send()


def prefill_part(plen, prompt_q, kv, prompt_out):
    position_of = lax.broadcasted_iota(jnp.int32, (C, KEYS), 1)
    own_row = lax.broadcasted_iota(jnp.int32, (C, KEYS), 0)
    usable = (position_of < plen[0]) | ((position_of >= PRE) & (position_of - PRE <= own_row))
    for c in range(2):
        keys = kv[0, 0, :, c * HD : (c + 1) * HD]
        values = kv[0, 1, :, c * HD : (c + 1) * HD]
        for g in range(PER_KV):
            columns = slice((c * PER_KV + g) * HD, (c * PER_KV + g + 1) * HD)
            scores = nt_dot(prompt_q[0, :, columns], keys) * SCALE
            scores = jnp.where(usable, scores, NEGATIVE)
            highest = jnp.max(scores, axis=-1, keepdims=True)
            terms = jnp.where(usable, jnp.exp(scores - highest), 0.0)
            total = jnp.sum(terms, axis=-1, keepdims=True)
            weighted = dot(terms.astype(BF16), values)
            prompt_out[0, :, columns] = (weighted / total).astype(BF16)


def local_part(lengths, q, cache, fresh, acc, stats):
    all_rows = KVH * ROWS
    row = lax.broadcasted_iota(jnp.int32, (all_rows, LOCAL_KEYS), 0)
    col = lax.broadcasted_iota(jnp.int32, (all_rows, LOCAL_KEYS), 1)
    in_cache = col < KVH * LOC
    head = row // ROWS
    cache_ok = in_cache & (col // LOC == head)
    fresh_col = col - KVH * LOC
    fresh_ok = (~in_cache) & (fresh_col // STEPS == head) & (fresh_col % STEPS <= row % STEPS)
    rank = jnp.where(cache_ok, col % LOC, jnp.where(fresh_ok, -1, 2 * LOC))
    lane = lax.broadcasted_iota(jnp.int32, (all_rows, 128), 1)

    def body(s, table):
        queries = q[s].reshape(all_rows, HD)
        keys = jnp.concatenate(
            [cache[s, 0, :, h * HD : (h + 1) * HD] for h in range(KVH)] + [fresh[s, 0]], axis=0
        )
        values = jnp.concatenate(
            [cache[s, 1, :, h * HD : (h + 1) * HD] for h in range(KVH)] + [fresh[s, 1]], axis=0
        )
        usable = rank < lengths[s]
        scores = jnp.where(usable, nt_dot(queries, keys) * SCALE, NEGATIVE)
        highest = jnp.max(scores, axis=-1, keepdims=True)
        terms = jnp.where(usable, jnp.exp(scores - highest), 0.0)
        total = jnp.sum(terms, axis=-1, keepdims=True)
        acc[s] = dot(terms.astype(BF16), values)
        table = jnp.where(lane == s, highest, table)
        return jnp.where(lane == s + 64, total, table)

    stats[...] = lax.fori_loop(0, SEQ, body, jnp.zeros((all_rows, 128), F32))


def home_kernel(plen, lengths, prompt_q, kv, q, cache, fresh, prompt_out, acc, stats):
    prefill_part(plen, prompt_q, kv, prompt_out)
    local_part(lengths, q, cache, fresh, acc, stats)


def remote_part(ring, sources, ka, kb, qg, ro, rs):
    lane = lax.broadcasted_iota(jnp.int32, (ROWS, 128), 1)
    group = 8

    def one(s, table):
        prompt = sources[ring * SEQ + s]
        where_at = lax.rem(prompt, NC) * (SLOTS * NZH // NC) + prompt // NC
        slot = where_at // NZH
        half = lax.rem(where_at, NZH)
        keys = ka[slot, half]
        values = kb[slot, half, 0:KEYS]
        bias = kb[slot, half, KEYS:].astype(F32)
        scores = nt_dot(qg[ring, s], keys) * SCALE
        prefix = scores[:, 0:PRE] + bias
        stretch = scores[:, PRE:]
        highest = jnp.maximum(
            jnp.max(prefix, axis=-1, keepdims=True), jnp.max(stretch, axis=-1, keepdims=True)
        )
        terms = jnp.concatenate([jnp.exp(prefix - highest), jnp.exp(stretch - highest)], axis=1)
        total = jnp.sum(terms, axis=-1, keepdims=True)
        ro[ring, s] = (dot(terms.astype(BF16), values) / total).astype(BF16)
        table = jnp.where(lane == s, highest, table)
        return jnp.where(lane == s + 64, total, table)

    def body(block, table):
        for i in range(group):
            table = one(block * group + i, table)
        return table

    rs[ring] = lax.fori_loop(0, SEQ // group, body, jnp.zeros((ROWS, 128), F32))


def remote_kernel(sources, ka, kb, qg, ro, rs):
    def body(ring, carry):
        remote_part(ring, sources, ka, kb, qg, ro, rs)
        return carry

    lax.fori_loop(0, RING, body, 0)


def return_kernel(ro, rs, bo, bs, local, send, recv):
    x, y, zh, core, zl = position()
    ring = zh * NZL + zl
    peers = [ring_device(x, y, core, lax.rem(ring + d, RING)) for d in range(1, RING)]
    enter(peers)
    copies = []
    for d in range(1, RING):
        other = lax.rem(ring + d, RING)
        for i, (source, target) in enumerate(((ro, bo), (rs, bs))):
            copies.append(
                remote(
                    source.at[other], target.at[ring], send.at[i, d - 1], recv.at[i, d - 1],
                    peers[d - 1],
                )
            )
            copies[-1].start()
    own = [
        pltpu.make_async_copy(ro.at[ring], bo.at[ring], local.at[0]),
        pltpu.make_async_copy(rs.at[ring], bs.at[ring], local.at[1]),
    ]
    for copy in own:
        copy.start()
    for copy in own + copies:
        copy.wait()


def merge_part(ring, head, bo, bs, acc, stats, out):
    far = bs[ring]
    rows = slice(head * ROWS, (head + 1) * ROWS)
    near = stats[rows]
    far_sum = pltpu.roll(far, 64, 1)
    near_sum = pltpu.roll(near, 64, 1)
    peak = jnp.maximum(far, near)
    near_scale = jnp.exp(near - peak)
    far_share = far_sum * jnp.exp(far - peak)
    whole = far_share + near_sum * near_scale
    far_weight = far_share / whole
    near_weight = near_scale / whole
    for s in range(SEQ):
        merged = (
            far_weight[:, s : s + 1] * bo[ring, s].astype(F32)
            + near_weight[:, s : s + 1] * acc[s, rows]
        )
        out[s, head] = merged.astype(BF16)


def merge_kernel(bo, bs, acc, stats, out):
    for ring in range(RING):
        merge_part(ring, 2 * (ring % NZL) + ring // NZL, bo, bs, acc, stats, out)


def shards(
    prompt_q, prompt_kv, prefix_length, decode_q, decode_kv, fresh_kv, source_prompt, cache_length
):
    q = decode_q[0].reshape(SEQ, STEPS, HEADS, HD).transpose(0, 2, 1, 3)
    q = q.reshape(SEQ, KVH, ROWS, HD)
    fresh = fresh_kv[0].reshape(SEQ, 2, STEPS, KVH, HD).transpose(0, 1, 3, 2, 4)
    fresh = fresh.reshape(SEQ, 2, KVH * STEPS, HD)
    src = jnp.pad(source_prompt[0, :, 0][None, :], ((0, 0), (0, 128 - SEQ)))
    vmem = pl.BlockSpec(memory_space=VMEM)
    smem = pl.BlockSpec(memory_space=pltpu.SMEM)
    anys = pl.BlockSpec(memory_space=pl.ANY)
    shape = jax.ShapeDtypeStruct
    sem = pltpu.SemaphoreType.DMA
    ka, kb, qg, srcg = pl.pallas_call(
        gather_kernel,
        out_shape=(
            shape((SLOTS, NZH, KEYS, HD), BF16),
            shape((SLOTS, NZH, KEYS + 16, HD), BF16),
            shape((RING, SEQ, ROWS, HD), BF16),
            shape((RING, 1, 128), jnp.int32),
        ),
        in_specs=[smem, vmem, anys, anys],
        out_specs=[anys] * 4,
        scratch_shapes=[
            VMEM((2, KEYS, HD), BF16),
            VMEM((2, KEYS + 16, HD), BF16),
            sem((4,)),
            sem((2,)),
            sem((RING - 1,)),
            sem((RING - 1,)),
            sem((RING - 1,)),
            sem((RING - 1,)),
            sem((2, 3)),
            sem((2, 3)),
            sem((2, 4, 3)),
            sem((2, 4, 3)),
            sem((2, 4, 4)),
            sem((2, 4, 4)),
            sem((2,)),
        ],
        compiler_params=pltpu.CompilerParams(
            collective_id=0, has_side_effects=True, vmem_limit_bytes=8 * MIB
        ),
        name="gather",
    )(prefix_length, prompt_kv, q, src)

    prompt_out, acc, stats = pl.pallas_call(
        home_kernel,
        out_shape=(
            shape((1, C, 2 * PER_KV * HD), BF16),
            shape((SEQ, KVH * ROWS, HD), F32),
            shape((KVH * ROWS, 128), F32),
        ),
        in_specs=[smem, smem, vmem, vmem, vmem, vmem, vmem],
        out_specs=[vmem] * 3,
        compiler_params=pltpu.CompilerParams(vmem_limit_bytes=32 * MIB),
        name="home",
    )(prefix_length, cache_length[0], prompt_q, prompt_kv, q, decode_kv[0], fresh)

    sources = srcg[:, 0, :SEQ].reshape(RING * SEQ)
    ro, rs = pl.pallas_call(
        remote_kernel,
        out_shape=(
            shape((RING, SEQ, ROWS, HD), BF16),
            shape((RING, ROWS, 128), F32),
        ),
        in_specs=[smem, vmem, vmem, vmem],
        out_specs=[vmem] * 2,
        compiler_params=pltpu.CompilerParams(vmem_limit_bytes=32 * MIB),
        name="attend",
    )(sources, ka, kb, qg)

    bo, bs = pl.pallas_call(
        return_kernel,
        out_shape=(
            shape((RING, SEQ, ROWS, HD), BF16),
            shape((RING, ROWS, 128), F32),
        ),
        in_specs=[anys] * 2,
        out_specs=[anys] * 2,
        scratch_shapes=[sem((2,)), sem((2, RING - 1)), sem((2, RING - 1))],
        compiler_params=pltpu.CompilerParams(
            collective_id=1, has_side_effects=True, vmem_limit_bytes=8 * MIB
        ),
        name="giveback",
    )(ro, rs)

    out = pl.pallas_call(
        merge_kernel,
        out_shape=shape((SEQ, KVH, ROWS, HD), BF16),
        in_specs=[vmem] * 4,
        out_specs=vmem,
        compiler_params=pltpu.CompilerParams(vmem_limit_bytes=32 * MIB),
        name="merge",
    )(bo, bs, acc, stats)
    out = out.reshape(SEQ, HEADS, STEPS, HD).transpose(0, 2, 1, 3)
    return prompt_out, out.reshape(1, SEQ, STEPS, HEADS * HD)


def solution(mesh):
    return jax.shard_map(
        shards,
        mesh=mesh,
        in_specs=(
            P("role", None, "tp"),
            P("role", None, None, "tp"),
            P("role"),
            P("role", "tp", None, None),
            P("role", "tp", None, None, None),
            P("role", "tp", None, None, None),
            P("role", "tp", None),
            P("role", "tp"),
        ),
        out_specs=(P("role", None, "tp"), P("role", "tp", None, None)),
        check_vma=False,
    )
```

```python
import math

import jax
import jax.numpy as jnp
from jax import lax
from jax.experimental import pallas as pl
from jax.experimental.pallas import tpu as pltpu
from jax.sharding import PartitionSpec as P

HEADS = 64
KVH = 8
PER_KV = HEADS // KVH
HD = 128
C = 64
PRE = 128
KEYS = PRE + C
LOC = 16
SEQ = 32
STEPS = 2
ROWS = PER_KV * STEPS
NX, NY, NZH, NC, NZL = 4, 4, 2, 2, 4
RING = NZH * NZL
SLOTS = NC * NX * NY
SCALE = 1.0 / math.sqrt(HD)
NEGATIVE = -1e30
LOCAL_KEYS = KVH * (LOC + STEPS)

F32 = jnp.float32
BF16 = jnp.bfloat16
VMEM = pltpu.VMEM
MIB = 1024 * 1024


def position():
    role = lax.axis_index("role")
    z_lo = lax.axis_index("tp")
    core = lax.rem(role, NC)
    z_hi = lax.rem(role // NC, NZH)
    y = lax.rem(role // (NC * NZH), NY)
    x = role // (NC * NZH * NY)
    return x, y, z_hi, core, z_lo


def device(x, y, z_hi, core, z_lo):
    return (((x * NY + y) * NZH + z_hi) * NC + core, z_lo)


def ring_device(x, y, core, ring):
    return device(x, y, ring // NZL, core, lax.rem(ring, NZL))


def ring_head(ring):
    return 2 * lax.rem(ring, NZL) + ring // NZL


def slot_of(x, y, core):
    return (core * NX + x) * NY + y


def nt_dot(a, b):
    return lax.dot_general(a, b, (((1,), (1,)), ((), ())), preferred_element_type=F32)


def dot(a, b):
    return jnp.dot(a, b, preferred_element_type=F32)


def enter(peers):
    barrier = pltpu.get_barrier_semaphore()
    for peer in peers:
        pl.semaphore_signal(barrier, inc=1, device_id=peer, device_id_type=pl.DeviceIdType.MESH)
    pl.semaphore_wait(barrier, len(peers))


def remote(src, dst, send, recv, peer):
    return pltpu.make_async_remote_copy(
        src_ref=src,
        dst_ref=dst,
        send_sem=send,
        recv_sem=recv,
        device_id=peer,
        device_id_type=pl.DeviceIdType.MESH,
    )


def prefill_part(c, plen, prompt_q, blk_a, blk_b, prompt_out):
    position_of = lax.broadcasted_iota(jnp.int32, (C, KEYS), 1)
    own_row = lax.broadcasted_iota(jnp.int32, (C, KEYS), 0)
    usable = (position_of < plen[0]) | ((position_of >= PRE) & (position_of - PRE <= own_row))
    keys = blk_a[c]
    values = blk_b[c, 0:KEYS]
    for g in range(PER_KV):
        columns = slice((c * PER_KV + g) * HD, (c * PER_KV + g + 1) * HD)
        scores = nt_dot(prompt_q[0, :, columns], keys) * SCALE
        scores = jnp.where(usable, scores, NEGATIVE)
        highest = jnp.max(scores, axis=-1, keepdims=True)
        terms = jnp.where(usable, jnp.exp(scores - highest), 0.0)
        total = jnp.sum(terms, axis=-1, keepdims=True)
        weighted = dot(terms.astype(BF16), values)
        prompt_out[0, :, columns] = (weighted / total).astype(BF16)


def local_part(first, last, lengths, q, cache, fresh, acc, stats):
    all_rows = KVH * ROWS
    row = lax.broadcasted_iota(jnp.int32, (all_rows, LOCAL_KEYS), 0)
    col = lax.broadcasted_iota(jnp.int32, (all_rows, LOCAL_KEYS), 1)
    in_cache = col < KVH * LOC
    head = row // ROWS
    cache_ok = in_cache & (col // LOC == head)
    fresh_col = col - KVH * LOC
    fresh_ok = (~in_cache) & (fresh_col // STEPS == head) & (fresh_col % STEPS <= row % STEPS)
    rank = jnp.where(cache_ok, col % LOC, jnp.where(fresh_ok, -1, 2 * LOC))
    lane = lax.broadcasted_iota(jnp.int32, (all_rows, 128), 1)
    group = 2

    def rows_of(s, which):
        return jnp.concatenate(
            [cache[s, which, :, h * HD : (h + 1) * HD] for h in range(KVH)] + [fresh[s, which]],
            axis=0,
        )

    def body(block, table):
        seqs = [block * group + i for i in range(group)]
        usable = [rank < lengths[s] for s in seqs]
        scores = [nt_dot(q[s].reshape(all_rows, HD), rows_of(s, 0)) for s in seqs]
        scores = [jnp.where(u, x * SCALE, NEGATIVE) for u, x in zip(usable, scores)]
        highest = [jnp.max(x, axis=-1, keepdims=True) for x in scores]
        terms = [
            jnp.where(u, jnp.exp(x - h), 0.0) for u, x, h in zip(usable, scores, highest)
        ]
        total = [jnp.sum(x, axis=-1, keepdims=True) for x in terms]
        weighted = [dot(x.astype(BF16), rows_of(s, 1)) for x, s in zip(terms, seqs)]
        for i, s in enumerate(seqs):
            acc[s] = weighted[i]
            table = jnp.where(lane == s, highest[i], table)
            table = jnp.where(lane == s + 64, total[i], table)
        return table

    start = jnp.zeros((all_rows, 128), F32) if first == 0 else stats[...]
    stats[...] = lax.fori_loop(first // group, last // group, body, start)


def remote_part(ring, sources, ka, kb, qg, ro, rs):
    lane = lax.broadcasted_iota(jnp.int32, (ROWS, 128), 1)
    group = 16

    def body(block, table):
        seqs = [block * group + i for i in range(group)]
        places = []
        for s in seqs:
            prompt = sources[ring, 0, s]
            slot = lax.rem(prompt, NC) * (SLOTS // NC) + prompt // (NC * NZH)
            places.append((slot, lax.rem(prompt // NC, NZH)))
        scores = jnp.concatenate(
            [nt_dot(qg[ring, s], ka[slot, half]) for s, (slot, half) in zip(seqs, places)], axis=0
        )
        scores = scores * SCALE
        bias = jnp.concatenate([kb[slot, half, KEYS:] for slot, half in places], axis=0)
        prefix = scores[:, 0:PRE] + bias.astype(F32)
        stretch = scores[:, PRE:]
        highest = jnp.maximum(
            jnp.max(prefix, axis=-1, keepdims=True), jnp.max(stretch, axis=-1, keepdims=True)
        )
        terms = jnp.concatenate([jnp.exp(prefix - highest), jnp.exp(stretch - highest)], axis=1)
        total = jnp.sum(terms, axis=-1, keepdims=True)
        weights = terms.astype(BF16)
        for i, (s, (slot, half)) in enumerate(zip(seqs, places)):
            rows = slice(i * ROWS, (i + 1) * ROWS)
            weighted = dot(weights[rows], kb[slot, half, 0:KEYS])
            ro[ring, s] = (weighted / total[rows]).astype(BF16)
            table = jnp.where(lane == s, highest[rows], table)
            table = jnp.where(lane == s + 64, total[rows], table)
        return table

    rs[ring] = lax.fori_loop(0, SEQ // group, body, jnp.zeros((ROWS, 128), F32))


def merge_part(ring, bo, bs, acc, stats, out):
    head = ring_head(ring)
    far = bs[ring]
    rows = pl.ds(pl.multiple_of(head * ROWS, ROWS), ROWS)
    near = stats[rows]
    far_sum = pltpu.roll(far, 64, 1)
    near_sum = pltpu.roll(near, 64, 1)
    peak = jnp.maximum(far, near)
    near_scale = jnp.exp(near - peak)
    far_share = far_sum * jnp.exp(far - peak)
    whole = far_share + near_sum * near_scale
    far_weight = far_share / whole
    near_weight = near_scale / whole
    for s in range(SEQ):
        merged = (
            far_weight[:, s : s + 1] * bo[ring, s].astype(F32)
            + near_weight[:, s : s + 1] * acc[s, rows]
        )
        out[s, head] = merged.astype(BF16)


def kernel(
    plen, lengths, prompt_q_hbm, kv, q, cache_hbm, fresh_hbm, src, prompt_out, out,
    blk_a, blk_b, ka, kb, qg, srcg, sources, ro, rs, bo, bs, acc, stats,
    prompt_q, q_own, cache, fresh, load, local,
    send_q, recv_q, send_s, recv_s, send_f, recv_f, send_1, recv_1, send_2, recv_2, send_c, recv_c,
    send_o, recv_o, send_t, recv_t,
):
    x, y, zh, core, zl = position()
    ring = zh * NZL + zl
    sibling = device(x, y, zh, 1 - core, zl)
    ring_peers = [ring_device(x, y, core, lax.rem(ring + d, RING)) for d in range(1, RING)]
    x_peers = [device(lax.rem(x + d, NX), y, zh, core, zl) for d in range(1, NX)]
    y_peers = [device(x, lax.rem(y + d, NY), zh, core, zl) for d in range(1, NY)]

    blocks = []
    for half in range(2):
        columns = slice(half * HD, (half + 1) * HD)
        blocks.append(
            pltpu.make_async_copy(kv.at[0, 0, :, columns], blk_a.at[half], load.at[half])
        )
        blocks.append(
            pltpu.make_async_copy(
                kv.at[0, 1, :, columns], blk_b.at[half, 0:KEYS], load.at[2 + half]
            )
        )
    loads = [
        pltpu.make_async_copy(prompt_q_hbm, prompt_q, load.at[4]),
        pltpu.make_async_copy(q, q_own, load.at[5]),
        pltpu.make_async_copy(cache_hbm, cache, load.at[6]),
        pltpu.make_async_copy(fresh_hbm, fresh, load.at[7]),
    ]
    for copy in blocks:
        copy.start()
    row_bias = jnp.where(
        lax.broadcasted_iota(jnp.int32, (16, PRE), 1) < plen[0], 0.0, NEGATIVE
    ).astype(BF16)
    for half in range(2):
        blk_b[half, KEYS:] = row_bias
    enter(ring_peers + x_peers + y_peers + [sibling])
    for copy in blocks:
        copy.wait()

    mine = slot_of(x, y, core)
    antipode = ring_peers[RING // 2 - 1]
    far_copies = [
        remote(blk.at[1 - zh], dst.at[mine, zh], send_f.at[i], recv_f.at[i], antipode)
        for i, (blk, dst) in enumerate(((blk_a, ka), (blk_b, kb)))
    ]
    for copy in far_copies:
        copy.start()
    local_copies = [
        pltpu.make_async_copy(blk_a.at[zh], ka.at[mine, zh], local.at[0]),
        pltpu.make_async_copy(blk_b.at[zh], kb.at[mine, zh], local.at[1]),
        pltpu.make_async_copy(q.at[:, ring_head(ring)], qg.at[ring], local.at[2]),
        pltpu.make_async_copy(src, srcg.at[ring], local.at[3]),
    ]
    for copy in local_copies:
        copy.start()
    q_copies = []
    for d in (4, 3, 5, 2, 6, 1, 7):
        other = lax.rem(ring + d, RING)
        q_copies.append(
            remote(src, srcg.at[ring], send_s.at[d - 1], recv_s.at[d - 1], ring_peers[d - 1])
        )
        q_copies.append(
            remote(
                q.at[:, ring_head(other)],
                qg.at[ring],
                send_q.at[d - 1],
                recv_q.at[d - 1],
                ring_peers[d - 1],
            )
        )
    for copy in q_copies:
        copy.start()
    for copy in loads:
        copy.start()

    loads[0].wait()
    prefill_part(0, plen, prompt_q, blk_a, blk_b, prompt_out)
    local_copies[0].wait()
    local_copies[1].wait()
    for copy in far_copies:
        copy.wait_recv()

    paths = ((ka, x_peers, y_peers), (kb, y_peers, x_peers))

    def slot_at(path, first, second):
        if path == 0:
            return slot_of(lax.rem(x + NX - first, NX), lax.rem(y + NY - second, NY), core)
        return slot_of(lax.rem(x + NX - second, NX), lax.rem(y + NY - first, NY), core)

    sent = []

    def push(ref, slot, send, recv, peer):
        copy = remote(ref.at[slot], ref.at[slot], send, recv, peer)
        copy.start()
        sent.append(copy)

    firsts = [[], []]
    seconds = [[], []]
    sides = []
    for path, (ref, first_peers, second_peers) in enumerate(paths):
        for d in range(1, 4):
            push(ref, mine, send_1.at[path, d - 1], recv_1.at[path, d - 1], first_peers[d - 1])
            firsts[path].append(sent[-1])
    for d in range(4):
        for path, (ref, first_peers, second_peers) in enumerate(paths):
            if d > 0:
                firsts[path][d - 1].wait_recv()
            slot = slot_at(path, d, 0)
            for e in range(1, 4):
                push(
                    ref, slot, send_2.at[path, d, e - 1], recv_2.at[path, d, e - 1],
                    second_peers[e - 1],
                )
                seconds[path].append(sent[-1])
            push(ref, slot, send_c.at[path, d, 0], recv_c.at[path, d, 0], sibling)
            sides.append(sent[-1])
        if d == 0:
            prefill_part(1, plen, prompt_q, blk_a, blk_b, prompt_out)
    for copy in loads[1:]:
        copy.wait()
    for d in range(4):
        local_part(d * 8, d * 8 + 8, lengths, q_own, cache, fresh, acc, stats)
        for path, (ref, first_peers, second_peers) in enumerate(paths):
            for e in range(1, 4):
                seconds[path][d * 3 + e - 1].wait_recv()
                push(
                    ref, slot_at(path, d, e), send_c.at[path, d, e], recv_c.at[path, d, e], sibling
                )
                sides.append(sent[-1])
    for copy in q_copies:
        copy.wait_recv()
    local_copies[2].wait()
    local_copies[3].wait()
    place = pltpu.make_async_copy(srcg, sources, local.at[4])
    place.start()
    place.wait()
    for copy in sides:
        copy.wait_recv()

    def answers(d):
        other = lax.rem(ring + d, RING)
        return [
            remote(
                ro.at[other], bo.at[ring], send_o.at[d], recv_o.at[d],
                ring_device(x, y, core, other),
            ),
            remote(
                rs.at[other], bs.at[ring], send_t.at[d], recv_t.at[d],
                ring_device(x, y, core, other),
            ),
        ]

    def distance(k):
        return RING // 2 + (1 - 2 * lax.rem(k, 2)) * ((k + 1) // 2)

    def answer(k, carry):
        d = distance(k)
        remote_part(lax.rem(ring + d, RING), sources, ka, kb, qg, ro, rs)

        @pl.when(k < RING - 1)
        def _():
            for copy in answers(d):
                copy.start()

        return carry

    lax.fori_loop(0, RING, answer, 0)
    bo[ring] = ro[ring]
    bs[ring] = rs[ring]

    def merge(k, carry):
        d = distance(k)

        @pl.when(k < RING - 1)
        def _():
            for copy in answers(d):
                copy.wait()

        merge_part(lax.rem(ring + RING - d, RING), bo, bs, acc, stats, out)
        return carry

    lax.fori_loop(0, RING, merge, 0)
    for copy in q_copies:
        copy.wait_send()
    for copy in far_copies:
        copy.wait_send()
    for copy in sent:
        copy.wait_send()


def shards(
    prompt_q, prompt_kv, prefix_length, decode_q, decode_kv, fresh_kv, source_prompt, cache_length
):
    q = decode_q[0].reshape(SEQ, STEPS, HEADS, HD).transpose(0, 2, 1, 3)
    q = q.reshape(SEQ, KVH, ROWS, HD)
    fresh = fresh_kv[0].reshape(SEQ, 2, STEPS, KVH, HD).transpose(0, 1, 3, 2, 4)
    fresh = fresh.reshape(SEQ, 2, KVH * STEPS, HD)
    src = jnp.pad(source_prompt[0, :, 0][None, :], ((0, 0), (0, 128 - SEQ)))
    vmem = pl.BlockSpec(memory_space=VMEM)
    smem = pl.BlockSpec(memory_space=pltpu.SMEM)
    anys = pl.BlockSpec(memory_space=pl.ANY)
    shape = jax.ShapeDtypeStruct
    sem = pltpu.SemaphoreType.DMA
    prompt_out, out = pl.pallas_call(
        kernel,
        out_shape=(
            shape((1, C, 2 * PER_KV * HD), BF16),
            shape((SEQ, KVH, ROWS, HD), BF16),
        ),
        in_specs=[smem, smem, anys, anys, anys, anys, anys, anys],
        out_specs=[vmem] * 2,
        scratch_shapes=[
            VMEM((2, KEYS, HD), BF16),
            VMEM((2, KEYS + 16, HD), BF16),
            VMEM((SLOTS, NZH, KEYS, HD), BF16),
            VMEM((SLOTS, NZH, KEYS + 16, HD), BF16),
            VMEM((RING, SEQ, ROWS, HD), BF16),
            VMEM((RING, 1, 128), jnp.int32),
            pltpu.SMEM((RING, 1, 128), jnp.int32),
            VMEM((RING, SEQ, ROWS, HD), BF16),
            VMEM((RING, ROWS, 128), F32),
            VMEM((RING, SEQ, ROWS, HD), BF16),
            VMEM((RING, ROWS, 128), F32),
            VMEM((SEQ, KVH * ROWS, HD), F32),
            VMEM((KVH * ROWS, 128), F32),
            VMEM((1, C, 2 * PER_KV * HD), BF16),
            VMEM((SEQ, KVH, ROWS, HD), BF16),
            VMEM((SEQ, 2, LOC, KVH * HD), BF16),
            VMEM((SEQ, 2, KVH * STEPS, HD), BF16),
            sem((8,)),
            sem((5,)),
        ]
        + [sem((RING - 1,))] * 4
        + [sem((2,))] * 2
        + [sem((2, 3))] * 2
        + [sem((2, 4, 3))] * 2
        + [sem((2, 4, 4))] * 2
        + [sem((RING,))] * 4,
        compiler_params=pltpu.CompilerParams(
            collective_id=0, has_side_effects=True, vmem_limit_bytes=58 * MIB
        ),
        name="attention",
    )(prefix_length, cache_length[0], prompt_q, prompt_kv, q, decode_kv[0], fresh, src)
    out = out.reshape(SEQ, HEADS, STEPS, HD).transpose(0, 2, 1, 3)
    return prompt_out, out.reshape(1, SEQ, STEPS, HEADS * HD)


def solution(mesh):
    return jax.shard_map(
        shards,
        mesh=mesh,
        in_specs=(
            P("role", None, "tp"),
            P("role", None, None, "tp"),
            P("role"),
            P("role", "tp", None, None),
            P("role", "tp", None, None, None),
            P("role", "tp", None, None, None),
            P("role", "tp", None),
            P("role", "tp"),
        ),
        out_specs=(P("role", None, "tp"), P("role", "tp", None, None)),
        check_vma=False,
    )
```

```python
import math

import jax
import jax.numpy as jnp
from jax import lax
from jax.experimental import pallas as pl
from jax.experimental.pallas import tpu as pltpu
from jax.sharding import PartitionSpec as P

HEADS = 64
KVH = 8
PER_KV = HEADS // KVH
HD = 128
C = 64
PRE = 128
KEYS = PRE + C
LOC = 16
SEQ = 32
STEPS = 2
ROWS = PER_KV * STEPS
NX, NY, NZH, NC, NZL = 4, 4, 2, 2, 4
RING = NZH * NZL
SLOTS = NC * NX * NY
SCALE = 1.0 / math.sqrt(HD)
NEGATIVE = -1e30
PARTS = 4
LOCAL_KEYS = KVH * (LOC + STEPS)

F32 = jnp.float32
BF16 = jnp.bfloat16
VMEM = pltpu.VMEM
MIB = 1024 * 1024


def position():
    role = lax.axis_index("role")
    z_lo = lax.axis_index("tp")
    core = lax.rem(role, NC)
    z_hi = lax.rem(role // NC, NZH)
    y = lax.rem(role // (NC * NZH), NY)
    x = role // (NC * NZH * NY)
    return x, y, z_hi, core, z_lo


def device(x, y, z_hi, core, z_lo):
    return (((x * NY + y) * NZH + z_hi) * NC + core, z_lo)


def ring_device(x, y, core, ring):
    return device(x, y, ring // NZL, core, lax.rem(ring, NZL))


def ring_head(ring):
    return 2 * lax.rem(ring, NZL) + ring // NZL


def slot_of(x, y, core):
    return (core * NX + x) * NY + y


def nt_dot(a, b):
    return lax.dot_general(a, b, (((1,), (1,)), ((), ())), preferred_element_type=F32)


def dot(a, b):
    return jnp.dot(a, b, preferred_element_type=F32)


def enter(peers):
    barrier = pltpu.get_barrier_semaphore()
    for peer in peers:
        pl.semaphore_signal(barrier, inc=1, device_id=peer, device_id_type=pl.DeviceIdType.MESH)
    pl.semaphore_wait(barrier, len(peers))


def remote(src, dst, send, recv, peer):
    return pltpu.make_async_remote_copy(
        src_ref=src,
        dst_ref=dst,
        send_sem=send,
        recv_sem=recv,
        device_id=peer,
        device_id_type=pl.DeviceIdType.MESH,
    )


def prefill_part(c, plen, prompt_q, blk_a, blk_b, prompt_out):
    position_of = lax.broadcasted_iota(jnp.int32, (C, KEYS), 1)
    own_row = lax.broadcasted_iota(jnp.int32, (C, KEYS), 0)
    usable = (position_of < plen[0]) | ((position_of >= PRE) & (position_of - PRE <= own_row))
    keys = blk_a[c]
    values = blk_b[c, 0:KEYS]
    for g in range(PER_KV):
        columns = slice((c * PER_KV + g) * HD, (c * PER_KV + g + 1) * HD)
        scores = nt_dot(prompt_q[0, :, columns], keys) * SCALE
        scores = jnp.where(usable, scores, NEGATIVE)
        highest = jnp.max(scores, axis=-1, keepdims=True)
        terms = jnp.where(usable, jnp.exp(scores - highest), 0.0)
        total = jnp.sum(terms, axis=-1, keepdims=True)
        weighted = dot(terms.astype(BF16), values)
        prompt_out[0, :, columns] = (weighted / total).astype(BF16)


def local_part(first, last, lengths, q, cache, fresh, acc, stats):
    all_rows = KVH * ROWS
    row = lax.broadcasted_iota(jnp.int32, (all_rows, LOCAL_KEYS), 0)
    col = lax.broadcasted_iota(jnp.int32, (all_rows, LOCAL_KEYS), 1)
    in_cache = col < KVH * LOC
    head = row // ROWS
    cache_ok = in_cache & (col // LOC == head)
    fresh_col = col - KVH * LOC
    fresh_ok = (~in_cache) & (fresh_col // STEPS == head) & (fresh_col % STEPS <= row % STEPS)
    rank = jnp.where(cache_ok, col % LOC, jnp.where(fresh_ok, -1, 2 * LOC))
    lane = lax.broadcasted_iota(jnp.int32, (all_rows, 128), 1)
    group = 2

    def rows_of(s, which):
        return jnp.concatenate(
            [cache[s, which, :, h * HD : (h + 1) * HD] for h in range(KVH)] + [fresh[s, which]],
            axis=0,
        )

    def body(block, table):
        seqs = [block * group + i for i in range(group)]
        usable = [rank < lengths[s] for s in seqs]
        scores = [nt_dot(q[s].reshape(all_rows, HD), rows_of(s, 0)) for s in seqs]
        scores = [jnp.where(u, x * SCALE, NEGATIVE) for u, x in zip(usable, scores)]
        highest = [jnp.max(x, axis=-1, keepdims=True) for x in scores]
        terms = [
            jnp.where(u, jnp.exp(x - h), 0.0) for u, x, h in zip(usable, scores, highest)
        ]
        total = [jnp.sum(x, axis=-1, keepdims=True) for x in terms]
        weighted = [dot(x.astype(BF16), rows_of(s, 1)) for x, s in zip(terms, seqs)]
        for i, s in enumerate(seqs):
            acc[s] = weighted[i]
            table = jnp.where(lane == s, highest[i], table)
            table = jnp.where(lane == s + 64, total[i], table)
        return table

    start = jnp.zeros((all_rows, 128), F32) if first == 0 else stats[...]
    stats[...] = lax.fori_loop(first // group, last // group, body, start)


def remote_part(ring, sources, ka, kb, qg, ro, rs):
    lane = lax.broadcasted_iota(jnp.int32, (ROWS, 128), 1)
    group = 16

    def body(block, table):
        seqs = [block * group + i for i in range(group)]
        places = []
        for s in seqs:
            prompt = sources[ring, 0, s]
            slot = lax.rem(prompt, NC) * (SLOTS // NC) + prompt // (NC * NZH)
            places.append((slot, lax.rem(prompt // NC, NZH)))
        scores = jnp.concatenate(
            [nt_dot(qg[ring, s], ka[slot, half]) for s, (slot, half) in zip(seqs, places)], axis=0
        )
        scores = scores * SCALE
        bias = jnp.concatenate([kb[slot, half, KEYS:] for slot, half in places], axis=0)
        prefix = scores[:, 0:PRE] + bias.astype(F32)
        stretch = scores[:, PRE:]
        highest = jnp.maximum(
            jnp.max(prefix, axis=-1, keepdims=True), jnp.max(stretch, axis=-1, keepdims=True)
        )
        terms = jnp.concatenate([jnp.exp(prefix - highest), jnp.exp(stretch - highest)], axis=1)
        total = jnp.sum(terms, axis=-1, keepdims=True)
        weights = terms.astype(BF16)
        for i, (s, (slot, half)) in enumerate(zip(seqs, places)):
            rows = slice(i * ROWS, (i + 1) * ROWS)
            weighted = dot(weights[rows], kb[slot, half, 0:KEYS])
            ro[ring, s] = (weighted / total[rows]).astype(BF16)
            table = jnp.where(lane == s, highest[rows], table)
            table = jnp.where(lane == s + 64, total[rows], table)
        return table

    table = lax.fori_loop(0, SEQ // group, body, jnp.zeros((ROWS, 128), F32))
    rs[ring] = table[0:8] + pltpu.roll(table[8:16], SEQ, 1)


def merge_part(ring, bo, bs, acc, stats, out):
    head = ring_head(ring)
    packed = bs[ring]
    far = jnp.concatenate([packed, pltpu.roll(packed, 128 - SEQ, 1)], axis=0)
    rows = pl.ds(pl.multiple_of(head * ROWS, ROWS), ROWS)
    near = stats[rows]
    far_sum = pltpu.roll(far, 64, 1)
    near_sum = pltpu.roll(near, 64, 1)
    peak = jnp.maximum(far, near)
    near_scale = jnp.exp(near - peak)
    far_share = far_sum * jnp.exp(far - peak)
    whole = far_share + near_sum * near_scale
    far_weight = far_share / whole
    near_weight = near_scale / whole
    for s in range(SEQ):
        merged = (
            far_weight[:, s : s + 1] * bo[ring, s].astype(F32)
            + near_weight[:, s : s + 1] * acc[s, rows]
        )
        out[s, head] = merged.astype(BF16)


def kernel(
    plen, lengths, prompt_q_hbm, kv, q, cache_hbm, fresh_hbm, src, prompt_out, out,
    blk_a, blk_b, ka, kb, qg, srcg, sources, ro, rs, bo, bs, acc, stats,
    prompt_q, q_own, cache, fresh, load, local,
    send_q, recv_q, send_s, recv_s, send_f, recv_f, send_1, recv_1, send_2, recv_2, send_c, recv_c,
    send_o, recv_o, send_t, recv_t,
):
    x, y, zh, core, zl = position()
    ring = zh * NZL + zl
    sibling = device(x, y, zh, 1 - core, zl)
    ring_peers = [ring_device(x, y, core, lax.rem(ring + d, RING)) for d in range(1, RING)]
    x_peers = [device(lax.rem(x + d, NX), y, zh, core, zl) for d in range(1, NX)]
    y_peers = [device(x, lax.rem(y + d, NY), zh, core, zl) for d in range(1, NY)]

    blocks = []
    for half in range(2):
        columns = slice(half * HD, (half + 1) * HD)
        blocks.append(
            pltpu.make_async_copy(kv.at[0, 0, :, columns], blk_a.at[half], load.at[half])
        )
        blocks.append(
            pltpu.make_async_copy(
                kv.at[0, 1, :, columns], blk_b.at[half, 0:KEYS], load.at[2 + half]
            )
        )
    loads = [
        pltpu.make_async_copy(prompt_q_hbm, prompt_q, load.at[4]),
        pltpu.make_async_copy(q, q_own, load.at[5]),
        pltpu.make_async_copy(cache_hbm, cache, load.at[6]),
        pltpu.make_async_copy(fresh_hbm, fresh, load.at[7]),
    ]
    for copy in blocks:
        copy.start()
    row_bias = jnp.where(
        lax.broadcasted_iota(jnp.int32, (16, PRE), 1) < plen[0], 0.0, NEGATIVE
    ).astype(BF16)
    for half in range(2):
        blk_b[half, KEYS:] = row_bias
    enter(ring_peers + x_peers + y_peers + [sibling])
    for copy in blocks:
        copy.wait()

    mine = slot_of(x, y, core)
    antipode = ring_peers[RING // 2 - 1]
    far_copies = [
        remote(blk.at[1 - zh], dst.at[mine, zh], send_f.at[i], recv_f.at[i], antipode)
        for i, (blk, dst) in enumerate(((blk_a, ka), (blk_b, kb)))
    ]
    for copy in far_copies:
        copy.start()
    local_copies = [
        pltpu.make_async_copy(blk_a.at[zh], ka.at[mine, zh], local.at[0]),
        pltpu.make_async_copy(blk_b.at[zh], kb.at[mine, zh], local.at[1]),
        pltpu.make_async_copy(q.at[:, ring_head(ring)], qg.at[ring], local.at[2]),
        pltpu.make_async_copy(src, srcg.at[ring], local.at[3]),
    ]
    for copy in local_copies:
        copy.start()
    q_copies = []
    for d in (4, 3, 5, 2, 6, 1, 7):
        other = lax.rem(ring + d, RING)
        q_copies.append(
            remote(src, srcg.at[ring], send_s.at[d - 1], recv_s.at[d - 1], ring_peers[d - 1])
        )
        q_copies.append(
            remote(
                q.at[:, ring_head(other)],
                qg.at[ring],
                send_q.at[d - 1],
                recv_q.at[d - 1],
                ring_peers[d - 1],
            )
        )
    for copy in q_copies:
        copy.start()
    for copy in loads:
        copy.start()

    loads[0].wait()
    prefill_part(0, plen, prompt_q, blk_a, blk_b, prompt_out)
    local_copies[0].wait()
    local_copies[1].wait()
    for copy in far_copies:
        copy.wait_recv()

    paths = ((ka, x_peers, y_peers), (kb, y_peers, x_peers))

    def slot_at(path, first, second):
        if path == 0:
            return slot_of(lax.rem(x + NX - first, NX), lax.rem(y + NY - second, NY), core)
        return slot_of(lax.rem(x + NX - second, NX), lax.rem(y + NY - first, NY), core)

    sent = []

    def push(ref, slot, send, recv, peer):
        copy = remote(ref.at[slot], ref.at[slot], send, recv, peer)
        copy.start()
        sent.append(copy)

    firsts = [[], []]
    seconds = [[], []]
    sides = []
    for path, (ref, first_peers, second_peers) in enumerate(paths):
        for d in range(1, 4):
            push(ref, mine, send_1.at[path, d - 1], recv_1.at[path, d - 1], first_peers[d - 1])
            firsts[path].append(sent[-1])
    for d in range(4):
        for path, (ref, first_peers, second_peers) in enumerate(paths):
            if d > 0:
                firsts[path][d - 1].wait_recv()
            slot = slot_at(path, d, 0)
            for e in range(1, 4):
                push(
                    ref, slot, send_2.at[path, d, e - 1], recv_2.at[path, d, e - 1],
                    second_peers[e - 1],
                )
                seconds[path].append(sent[-1])
            push(ref, slot, send_c.at[path, d, 0], recv_c.at[path, d, 0], sibling)
            sides.append(sent[-1])
        if d == 0:
            prefill_part(1, plen, prompt_q, blk_a, blk_b, prompt_out)
    for copy in loads[1:]:
        copy.wait()
    for d in range(4):
        local_part(d * 8, d * 8 + 8, lengths, q_own, cache, fresh, acc, stats)
        for path, (ref, first_peers, second_peers) in enumerate(paths):
            for e in range(1, 4):
                seconds[path][d * 3 + e - 1].wait_recv()
                push(
                    ref, slot_at(path, d, e), send_c.at[path, d, e], recv_c.at[path, d, e], sibling
                )
                sides.append(sent[-1])
    for copy in q_copies:
        copy.wait_recv()
    local_copies[2].wait()
    local_copies[3].wait()
    place = pltpu.make_async_copy(srcg, sources, local.at[4])
    place.start()
    place.wait()
    for copy in sides:
        copy.wait_recv()

    def answers(d):
        other = lax.rem(ring + d, RING)
        return [
            remote(
                ro.at[other], bo.at[ring], send_o.at[d], recv_o.at[d],
                ring_device(x, y, core, other),
            ),
            remote(
                rs.at[other], bs.at[ring], send_t.at[d], recv_t.at[d],
                ring_device(x, y, core, other),
            ),
        ]

    def distance(k):
        return RING // 2 + (1 - 2 * lax.rem(k, 2)) * ((k + 1) // 2)

    def answer(k, carry):
        d = distance(k)
        remote_part(lax.rem(ring + d, RING), sources, ka, kb, qg, ro, rs)

        @pl.when(k < RING - 1)
        def _():
            for copy in answers(d):
                copy.start()

        return carry

    lax.fori_loop(0, RING, answer, 0)
    bo[ring] = ro[ring]
    bs[ring] = rs[ring]

    def merge(k, carry):
        d = distance(k)

        @pl.when(k < RING - 1)
        def _():
            for copy in answers(d):
                copy.wait()

        merge_part(lax.rem(ring + RING - d, RING), bo, bs, acc, stats, out)
        return carry

    lax.fori_loop(0, RING, merge, 0)
    for copy in q_copies:
        copy.wait_send()
    for copy in far_copies:
        copy.wait_send()
    for copy in sent:
        copy.wait_send()


def copy_kernel(a, b, out_a, out_b, stage_a, stage_b, sem_in, sem_out):
    loads = [pltpu.make_async_copy(a, stage_a, sem_in.at[PARTS])]
    stores = [pltpu.make_async_copy(stage_a, out_a, sem_out.at[PARTS])]
    for i in range(PARTS):
        rows = pl.ds(i * (SEQ // PARTS), SEQ // PARTS)
        loads.append(pltpu.make_async_copy(b.at[rows], stage_b.at[rows], sem_in.at[i]))
        stores.append(pltpu.make_async_copy(stage_b.at[rows], out_b.at[rows], sem_out.at[i]))
    for copy in loads:
        copy.start()
    for load, store in zip(loads, stores):
        load.wait()
        store.start()
    for copy in stores:
        copy.wait()


def shards(
    prompt_q, prompt_kv, prefix_length, decode_q, decode_kv, fresh_kv, source_prompt, cache_length
):
    q = decode_q[0].reshape(SEQ, STEPS, HEADS, HD).transpose(0, 2, 1, 3)
    q = q.reshape(SEQ, KVH, ROWS, HD)
    fresh = fresh_kv[0].reshape(SEQ, 2, STEPS, KVH, HD).transpose(0, 1, 3, 2, 4)
    fresh = fresh.reshape(SEQ, 2, KVH * STEPS, HD)
    src = source_prompt[0, :, 0][None, :]
    vmem = pl.BlockSpec(memory_space=VMEM)
    smem = pl.BlockSpec(memory_space=pltpu.SMEM)
    anys = pl.BlockSpec(memory_space=pl.ANY)
    shape = jax.ShapeDtypeStruct
    sem = pltpu.SemaphoreType.DMA
    prompt_out, out = pl.pallas_call(
        kernel,
        out_shape=(
            shape((1, C, 2 * PER_KV * HD), BF16),
            shape((SEQ, KVH, ROWS, HD), BF16),
        ),
        in_specs=[smem, smem, anys, anys, anys, anys, anys, anys],
        out_specs=[vmem] * 2,
        scratch_shapes=[
            VMEM((2, KEYS, HD), BF16),
            VMEM((2, KEYS + 16, HD), BF16),
            VMEM((SLOTS, NZH, KEYS, HD), BF16),
            VMEM((SLOTS, NZH, KEYS + 16, HD), BF16),
            VMEM((RING, SEQ, ROWS, HD), BF16),
            VMEM((RING, 1, SEQ), jnp.int32),
            pltpu.SMEM((RING, 1, SEQ), jnp.int32),
            VMEM((RING, SEQ, ROWS, HD), BF16),
            VMEM((RING, 8, 128), F32),
            VMEM((RING, SEQ, ROWS, HD), BF16),
            VMEM((RING, 8, 128), F32),
            VMEM((SEQ, KVH * ROWS, HD), F32),
            VMEM((KVH * ROWS, 128), F32),
            VMEM((1, C, 2 * PER_KV * HD), BF16),
            VMEM((SEQ, KVH, ROWS, HD), BF16),
            VMEM((SEQ, 2, LOC, KVH * HD), BF16),
            VMEM((SEQ, 2, KVH * STEPS, HD), BF16),
            sem((8,)),
            sem((5,)),
        ]
        + [sem((RING - 1,))] * 4
        + [sem((2,))] * 2
        + [sem((2, 3))] * 2
        + [sem((2, 4, 3))] * 2
        + [sem((2, 4, 4))] * 2
        + [sem((RING,))] * 4,
        compiler_params=pltpu.CompilerParams(
            collective_id=0, has_side_effects=True, vmem_limit_bytes=58 * MIB
        ),
        name="attention",
    )(prefix_length, cache_length[0], prompt_q, prompt_kv, q, decode_kv[0], fresh, src)
    prompt_out, out = pl.pallas_call(
        copy_kernel,
        out_shape=(shape(prompt_out.shape, BF16), shape(out.shape, BF16)),
        in_specs=[anys] * 2,
        out_specs=[anys] * 2,
        scratch_shapes=[
            VMEM(prompt_out.shape, BF16),
            VMEM(out.shape, BF16),
            sem((PARTS + 1,)),
            sem((PARTS + 1,)),
        ],
        name="place",
    )(prompt_out, out)
    out = out.reshape(SEQ, HEADS, STEPS, HD).transpose(0, 2, 1, 3)
    return prompt_out, out.reshape(1, SEQ, STEPS, HEADS * HD)


def solution(mesh):
    return jax.shard_map(
        shards,
        mesh=mesh,
        in_specs=(
            P("role", None, "tp"),
            P("role", None, None, "tp"),
            P("role"),
            P("role", "tp", None, None),
            P("role", "tp", None, None, None),
            P("role", "tp", None, None, None),
            P("role", "tp", None),
            P("role", "tp"),
        ),
        out_specs=(P("role", None, "tp"), P("role", "tp", None, None)),
        check_vma=False,
    )
```

```python
import math

import jax
import jax.numpy as jnp
from jax import lax
from jax.experimental import pallas as pl
from jax.experimental.pallas import tpu as pltpu
from jax.sharding import PartitionSpec as P

HEADS = 64
KVH = 8
PER_KV = HEADS // KVH
HD = 128
C = 64
PRE = 128
KEYS = PRE + C
LOC = 16
SEQ = 32
STEPS = 2
ROWS = PER_KV * STEPS
NX, NY, NZH, NC, NZL = 4, 4, 2, 2, 4
RING = NZH * NZL
SLOTS = NC * NX * NY
SCALE = 1.0 / math.sqrt(HD)
NEGATIVE = -1e30
PARTS = 4
LOCAL_KEYS = KVH * (LOC + STEPS)

F32 = jnp.float32
BF16 = jnp.bfloat16
VMEM = pltpu.VMEM
MIB = 1024 * 1024


def position():
    role = lax.axis_index("role")
    z_lo = lax.axis_index("tp")
    core = lax.rem(role, NC)
    z_hi = lax.rem(role // NC, NZH)
    y = lax.rem(role // (NC * NZH), NY)
    x = role // (NC * NZH * NY)
    return x, y, z_hi, core, z_lo


def device(x, y, z_hi, core, z_lo):
    return (((x * NY + y) * NZH + z_hi) * NC + core, z_lo)


def ring_device(x, y, core, ring):
    return device(x, y, ring // NZL, core, lax.rem(ring, NZL))


def ring_head(ring):
    return 2 * lax.rem(ring, NZL) + ring // NZL


def slot_of(x, y, core):
    return (core * NX + x) * NY + y


def nt_dot(a, b):
    return lax.dot_general(a, b, (((1,), (1,)), ((), ())), preferred_element_type=F32)


def dot(a, b):
    return jnp.dot(a, b, preferred_element_type=F32)


def enter(peers):
    barrier = pltpu.get_barrier_semaphore()
    for peer in peers:
        pl.semaphore_signal(barrier, inc=1, device_id=peer, device_id_type=pl.DeviceIdType.MESH)
    pl.semaphore_wait(barrier, len(peers))


def remote(src, dst, send, recv, peer):
    return pltpu.make_async_remote_copy(
        src_ref=src,
        dst_ref=dst,
        send_sem=send,
        recv_sem=recv,
        device_id=peer,
        device_id_type=pl.DeviceIdType.MESH,
    )


def prefill_part(c, plen, prompt_q, blk_a, blk_b, prompt_out):
    position_of = lax.broadcasted_iota(jnp.int32, (C, KEYS), 1)
    own_row = lax.broadcasted_iota(jnp.int32, (C, KEYS), 0)
    usable = (position_of < plen[0]) | ((position_of >= PRE) & (position_of - PRE <= own_row))
    keys = blk_a[c]
    values = blk_b[c, 0:KEYS]
    for g in range(PER_KV):
        columns = slice((c * PER_KV + g) * HD, (c * PER_KV + g + 1) * HD)
        scores = nt_dot(prompt_q[0, :, columns], keys) * SCALE
        scores = jnp.where(usable, scores, NEGATIVE)
        highest = jnp.max(scores, axis=-1, keepdims=True)
        terms = jnp.where(usable, jnp.exp(scores - highest), 0.0)
        total = jnp.sum(terms, axis=-1, keepdims=True)
        weighted = dot(terms.astype(BF16), values)
        prompt_out[0, :, columns] = (weighted / total).astype(BF16)


def local_part(first, last, lengths, q, cache, fresh, acc, stats):
    all_rows = KVH * ROWS
    row = lax.broadcasted_iota(jnp.int32, (all_rows, LOCAL_KEYS), 0)
    col = lax.broadcasted_iota(jnp.int32, (all_rows, LOCAL_KEYS), 1)
    in_cache = col < KVH * LOC
    head = row // ROWS
    cache_ok = in_cache & (col // LOC == head)
    fresh_col = col - KVH * LOC
    fresh_ok = (~in_cache) & (fresh_col // STEPS == head) & (fresh_col % STEPS <= row % STEPS)
    rank = jnp.where(cache_ok, col % LOC, jnp.where(fresh_ok, -1, 2 * LOC))
    lane = lax.broadcasted_iota(jnp.int32, (all_rows, 128), 1)
    group = 2

    def rows_of(s, which):
        return jnp.concatenate(
            [cache[s, which, :, h * HD : (h + 1) * HD] for h in range(KVH)] + [fresh[s, which]],
            axis=0,
        )

    def body(block, table):
        seqs = [block * group + i for i in range(group)]
        usable = [rank < lengths[s] for s in seqs]
        scores = [nt_dot(q[s].reshape(all_rows, HD), rows_of(s, 0)) for s in seqs]
        scores = [jnp.where(u, x * SCALE, NEGATIVE) for u, x in zip(usable, scores)]
        highest = [jnp.max(x, axis=-1, keepdims=True) for x in scores]
        terms = [
            jnp.where(u, jnp.exp(x - h), 0.0) for u, x, h in zip(usable, scores, highest)
        ]
        total = [jnp.sum(x, axis=-1, keepdims=True) for x in terms]
        weighted = [dot(x.astype(BF16), rows_of(s, 1)) for x, s in zip(terms, seqs)]
        for i, s in enumerate(seqs):
            acc[s] = weighted[i]
            table = jnp.where(lane == s, highest[i], table)
            table = jnp.where(lane == s + 64, total[i], table)
        return table

    start = jnp.zeros((all_rows, 128), F32) if first == 0 else stats[...]
    stats[...] = lax.fori_loop(first // group, last // group, body, start)


def remote_part(ring, sources, ka, kb, qg, ro, rs):
    lane = lax.broadcasted_iota(jnp.int32, (ROWS, 128), 1)
    group = 16

    def body(block, table):
        seqs = [block * group + i for i in range(group)]
        places = []
        for s in seqs:
            prompt = sources[ring, 0, s]
            slot = lax.rem(prompt, NC) * (SLOTS // NC) + prompt // (NC * NZH)
            places.append((slot, lax.rem(prompt // NC, NZH)))
        scores = jnp.concatenate(
            [nt_dot(qg[ring, s], ka[slot, half]) for s, (slot, half) in zip(seqs, places)], axis=0
        )
        scores = scores * SCALE
        bias = jnp.concatenate([kb[slot, half, KEYS:] for slot, half in places], axis=0)
        prefix = scores[:, 0:PRE] + bias.astype(F32)
        stretch = scores[:, PRE:]
        highest = jnp.maximum(
            jnp.max(prefix, axis=-1, keepdims=True), jnp.max(stretch, axis=-1, keepdims=True)
        )
        terms = jnp.concatenate([jnp.exp(prefix - highest), jnp.exp(stretch - highest)], axis=1)
        total = jnp.sum(terms, axis=-1, keepdims=True)
        weights = terms.astype(BF16)
        for i, (s, (slot, half)) in enumerate(zip(seqs, places)):
            rows = slice(i * ROWS, (i + 1) * ROWS)
            weighted = dot(weights[rows], kb[slot, half, 0:KEYS])
            ro[ring, s] = (weighted / total[rows]).astype(BF16)
            table = jnp.where(lane == s, highest[rows], table)
            table = jnp.where(lane == s + 64, total[rows], table)
        return table

    table = lax.fori_loop(0, SEQ // group, body, jnp.zeros((ROWS, 128), F32))
    rs[ring] = table[0:8] + pltpu.roll(table[8:16], SEQ, 1)


def merge_part(ring, bo, bs, acc, stats, out):
    head = ring_head(ring)
    packed = bs[ring]
    far = jnp.concatenate([packed, pltpu.roll(packed, 128 - SEQ, 1)], axis=0)
    rows = pl.ds(pl.multiple_of(head * ROWS, ROWS), ROWS)
    near = stats[rows]
    far_sum = pltpu.roll(far, 64, 1)
    near_sum = pltpu.roll(near, 64, 1)
    peak = jnp.maximum(far, near)
    near_scale = jnp.exp(near - peak)
    far_share = far_sum * jnp.exp(far - peak)
    whole = far_share + near_sum * near_scale
    far_weight = far_share / whole
    near_weight = near_scale / whole
    for s in range(SEQ):
        merged = (
            far_weight[:, s : s + 1] * bo[ring, s].astype(F32)
            + near_weight[:, s : s + 1] * acc[s, rows]
        )
        out[s, head] = merged.astype(BF16)


def kernel(
    plen, lengths, prompt_q_hbm, kv, q, cache_hbm, fresh_hbm, src, prompt_out, out,
    blk_a, blk_b, ka, kb, ka2, kb2, qg, srcg, sources, ro, rs, bo, bs, acc, stats,
    prompt_q, q_own, cache, fresh, load, local,
    send_q, recv_q, send_s, recv_s, send_f, recv_f, send_1, recv_1, send_2, recv_2, send_c, recv_c,
    send_o, recv_o, send_t, recv_t,
):
    x, y, zh, core, zl = position()
    ring = zh * NZL + zl
    opposite = lax.rem(ring + RING // 2, RING)
    sibling = device(x, y, zh, 1 - core, zl)
    ring_peers = [ring_device(x, y, core, lax.rem(ring + d, RING)) for d in range(1, RING)]
    x_peers = [device(lax.rem(x + d, NX), y, zh, core, zl) for d in range(1, NX)]
    y_peers = [device(x, lax.rem(y + d, NY), zh, core, zl) for d in range(1, NY)]

    blocks = []
    for half in range(2):
        columns = slice(half * HD, (half + 1) * HD)
        blocks.append(
            pltpu.make_async_copy(kv.at[0, 0, :, columns], blk_a.at[half], load.at[half])
        )
        blocks.append(
            pltpu.make_async_copy(
                kv.at[0, 1, :, columns], blk_b.at[half, 0:KEYS], load.at[2 + half]
            )
        )
    loads = [
        pltpu.make_async_copy(prompt_q_hbm, prompt_q, load.at[4]),
        pltpu.make_async_copy(q, q_own, load.at[5]),
        pltpu.make_async_copy(cache_hbm, cache, load.at[6]),
        pltpu.make_async_copy(fresh_hbm, fresh, load.at[7]),
    ]
    local_copies = [
        pltpu.make_async_copy(q.at[:, ring_head(ring)], qg.at[ring], local.at[0]),
        pltpu.make_async_copy(q.at[:, ring_head(opposite)], qg.at[opposite], local.at[1]),
        pltpu.make_async_copy(src, srcg.at[ring], local.at[2]),
    ]
    for copy in blocks + loads + local_copies:
        copy.start()
    row_bias = jnp.where(
        lax.broadcasted_iota(jnp.int32, (16, PRE), 1) < plen[0], 0.0, NEGATIVE
    ).astype(BF16)
    for half in range(2):
        blk_b[half, KEYS:] = row_bias
    for copy in blocks:
        copy.wait()
    mine = slot_of(x, y, core)
    ka[mine, zh] = blk_a[zh]
    kb[mine, zh] = blk_b[zh]
    ka2[mine, zh] = blk_a[1 - zh]
    kb2[mine, zh] = blk_b[1 - zh]
    enter(ring_peers + x_peers + y_peers + [sibling])

    antipode = ring_peers[RING // 2 - 1]
    far_copies = [
        remote(blk.at[head], dst.at[mine, zh], send_f.at[i], recv_f.at[i], antipode)
        for i, (blk, dst, head) in enumerate(
            ((blk_a, ka, 1 - zh), (blk_b, kb, 1 - zh), (blk_a, ka2, zh), (blk_b, kb2, zh))
        )
    ]
    for copy in far_copies[:2]:
        copy.start()

    def slot_at(path, first, second):
        dx, dy = (first, second) if path == 0 else (second, first)
        return slot_of(lax.rem(x + NX - dx, NX), lax.rem(y + NY - dy, NY), core)

    def along(path, phase, d):
        return (x_peers if (path + phase) % 2 == 0 else y_peers)[d - 1]

    streams = (
        (lambda slot: (ka.at[slot, zh], kb.at[slot, zh])),
        (lambda slot: (ka.at[slot, 1 - zh], kb.at[slot, 1 - zh])),
        (lambda slot: (ka2.at[slot], kb2.at[slot])),
    )
    pieces = ((), (), ((0, 1), (1, 3)))

    def part(stream, path, slot, piece):
        ref = streams[stream](slot)[path]
        return ref if piece is None else ref.at[piece]

    def first_copies(stream, path, way):
        if way != 2 or not pieces[stream]:
            ref = part(stream, path, mine, None)
            return [
                remote(
                    ref, ref, send_1.at[stream, path, way], recv_1.at[stream, path, way],
                    along(path, 0, way),
                )
            ]
        copies = []
        for piece, to in pieces[stream]:
            ref = part(stream, path, slot_at(path, to, 0), piece)
            i = 0 if to == 1 else 2
            copies.append(
                remote(
                    ref, ref, send_1.at[stream, path, i], recv_1.at[stream, path, i],
                    along(path, 0, to),
                )
            )
        return copies

    def second_copies(stream, path, d, way):
        if way != 2 or not pieces[stream]:
            ref = part(stream, path, slot_at(path, d, 0), None)
            return [
                remote(
                    ref, ref, send_2.at[stream, path, d, way], recv_2.at[stream, path, d, way],
                    along(path, 1, way),
                )
            ]
        copies = []
        for piece, to in pieces[stream]:
            ref = part(stream, path, slot_at(path, d, to), piece)
            i = 0 if to == 1 else 2
            copies.append(
                remote(
                    ref, ref, send_2.at[stream, path, d, i], recv_2.at[stream, path, d, i],
                    along(path, 1, to),
                )
            )
        return copies

    def side_copies(stream, path, d, e):
        ref = part(stream, path, slot_at(path, d, e), None)
        return [
            remote(
                ref, ref, send_c.at[stream, path, d, e], recv_c.at[stream, path, d, e], sibling
            )
        ]

    def start(copies):
        for copy in copies:
            copy.start()

    def arrived(copies):
        for copy in copies:
            copy.wait_recv()

    def gone(copies):
        for copy in copies:
            copy.wait_send()

    def begin(stream):
        for path in range(2):
            start(first_copies(stream, path, 1))
            start(first_copies(stream, path, 3))
            if not pieces[stream]:
                start(first_copies(stream, path, 2))

    def go_on(stream):
        if not pieces[stream]:
            return
        for path in range(2):
            for piece, to in pieces[stream]:
                arrived(first_copies(stream, path, to))
            start(first_copies(stream, path, 2))

    def spread(stream, d):
        passed = [to for piece, to in pieces[stream]]
        for path in range(2):
            if d > 0 and d not in passed:
                arrived(first_copies(stream, path, d))
            start(second_copies(stream, path, d, 1))
            start(second_copies(stream, path, d, 3))
            if not pieces[stream]:
                start(second_copies(stream, path, d, 2))
            start(side_copies(stream, path, d, 0))

    def go_on_second(stream, d):
        if not pieces[stream]:
            return
        for path in range(2):
            for piece, to in pieces[stream]:
                arrived(second_copies(stream, path, d, to))
            start(second_copies(stream, path, d, 2))
            for piece, to in pieces[stream]:
                start(side_copies(stream, path, d, to))

    def finish(stream, d):
        passed = [to for piece, to in pieces[stream]]
        for path in range(2):
            for way in (1, 3, 2):
                if way not in passed:
                    arrived(second_copies(stream, path, d, way))
                    start(side_copies(stream, path, d, way))

    def sides(stream):
        return [
            copy
            for path in range(2)
            for d in range(4)
            for e in range(4)
            for copy in side_copies(stream, path, d, e)
        ]

    def spreading(stream):
        copies = []
        for path in range(2):
            for way in (1, 3, 2):
                copies += first_copies(stream, path, way)
                for d in range(4):
                    copies += second_copies(stream, path, d, way)
        return copies

    def local_rows(first, last):
        local_part(first, last, lengths, q_own, cache, fresh, acc, stats)

    begin(0)
    spread(0, 0)
    q_copies = []
    src_copies = []
    for d in (3, 5, 2, 6, 1, 7):
        other = lax.rem(ring + d, RING)
        src_copies.append(
            remote(src, srcg.at[ring], send_s.at[d - 1], recv_s.at[d - 1], ring_peers[d - 1])
        )
        q_copies.append(
            remote(
                q.at[:, ring_head(other)],
                qg.at[ring],
                send_q.at[d - 1],
                recv_q.at[d - 1],
                ring_peers[d - 1],
            )
        )
    start(far_copies[2:])
    start(src_copies + q_copies)
    go_on(0)
    spread(0, 1)
    spread(0, 3)
    loads[0].wait()
    prefill_part(0, plen, prompt_q, blk_a, blk_b, prompt_out)
    spread(0, 2)
    arrived(far_copies[:2])
    begin(1)
    spread(1, 0)
    go_on_second(0, 0)
    for copy in loads[1:]:
        copy.wait()
    prefill_part(1, plen, prompt_q, blk_a, blk_b, prompt_out)
    go_on(1)
    spread(1, 1)
    spread(1, 3)
    go_on_second(0, 1)
    go_on_second(0, 3)
    spread(1, 2)
    arrived(far_copies[2:])
    begin(2)
    spread(2, 0)
    local_rows(0, 4)
    go_on_second(1, 0)
    go_on_second(0, 2)
    local_rows(4, 8)
    go_on_second(1, 1)
    go_on_second(1, 3)
    local_rows(8, 12)
    go_on_second(1, 2)
    local_rows(12, 16)
    for d in (0, 1, 3, 2):
        finish(0, d)
    local_rows(16, 24)
    arrived(src_copies)
    for copy in local_copies:
        copy.wait()
    srcg[opposite] = srcg[ring]
    place = pltpu.make_async_copy(srcg, sources, local.at[3])
    place.start()
    local_rows(24, 32)
    place.wait()
    for d in (0, 1, 3, 2):
        finish(1, d)
    go_on(2)
    spread(2, 1)
    spread(2, 3)
    arrived(q_copies)
    arrived(sides(0) + sides(1))

    def answers(d):
        other = lax.rem(ring + d, RING)
        return [
            remote(
                ro.at[other], bo.at[ring], send_o.at[d], recv_o.at[d],
                ring_device(x, y, core, other),
            ),
            remote(
                rs.at[other], bs.at[ring], send_t.at[d], recv_t.at[d],
                ring_device(x, y, core, other),
            ),
        ]

    def distance(k):
        return RING // 2 + (2 * lax.rem(k, 2) - 1) * (1 + k // 2)

    def answer(k, carry):
        d = distance(k)
        remote_part(lax.rem(ring + d, RING), sources, ka, kb, qg, ro, rs)

        @pl.when(k < RING - 2)
        def _():
            start(answers(d))

        @pl.when(k == 0)
        def _():
            spread(2, 2)

        @pl.when(k == 1)
        def _():
            go_on_second(2, 0)

        @pl.when(k == 3)
        def _():
            go_on_second(2, 1)
            go_on_second(2, 3)

        @pl.when(k == 4)
        def _():
            go_on_second(2, 2)

        return carry

    def merge(k, carry):
        d = distance(k)
        for copy in answers(d):
            copy.wait()
        merge_part(lax.rem(ring + RING - d, RING), bo, bs, acc, stats, out)
        return carry

    lax.fori_loop(0, RING - 1, answer, 0)
    for d in (0, 1, 3, 2):
        finish(2, d)
    lax.fori_loop(0, 2, merge, 0)
    arrived(sides(2))
    remote_part(opposite, sources, ka2, kb2, qg, ro, rs)
    for place_at in (ring, opposite):
        bo[place_at] = ro[place_at]
        bs[place_at] = rs[place_at]
        merge_part(place_at, bo, bs, acc, stats, out)
    lax.fori_loop(2, RING - 2, merge, 0)
    gone(q_copies + src_copies + far_copies)
    for stream in range(3):
        gone(spreading(stream) + sides(stream))


def copy_kernel(a, b, out_a, out_b, stage_a, stage_b, sem_in, sem_out):
    loads = [pltpu.make_async_copy(a, stage_a, sem_in.at[PARTS])]
    stores = [pltpu.make_async_copy(stage_a, out_a, sem_out.at[PARTS])]
    for i in range(PARTS):
        rows = pl.ds(i * (SEQ // PARTS), SEQ // PARTS)
        loads.append(pltpu.make_async_copy(b.at[rows], stage_b.at[rows], sem_in.at[i]))
        stores.append(pltpu.make_async_copy(stage_b.at[rows], out_b.at[rows], sem_out.at[i]))
    for copy in loads:
        copy.start()
    for load, store in zip(loads, stores):
        load.wait()
        store.start()
    for copy in stores:
        copy.wait()


def shards(
    prompt_q, prompt_kv, prefix_length, decode_q, decode_kv, fresh_kv, source_prompt, cache_length
):
    q = decode_q[0].reshape(SEQ, STEPS, HEADS, HD).transpose(0, 2, 1, 3)
    q = q.reshape(SEQ, KVH, ROWS, HD)
    fresh = fresh_kv[0].reshape(SEQ, 2, STEPS, KVH, HD).transpose(0, 1, 3, 2, 4)
    fresh = fresh.reshape(SEQ, 2, KVH * STEPS, HD)
    src = source_prompt[0, :, 0][None, :]
    vmem = pl.BlockSpec(memory_space=VMEM)
    smem = pl.BlockSpec(memory_space=pltpu.SMEM)
    anys = pl.BlockSpec(memory_space=pl.ANY)
    shape = jax.ShapeDtypeStruct
    sem = pltpu.SemaphoreType.DMA
    prompt_out, out = pl.pallas_call(
        kernel,
        out_shape=(
            shape((1, C, 2 * PER_KV * HD), BF16),
            shape((SEQ, KVH, ROWS, HD), BF16),
        ),
        in_specs=[smem, smem, anys, anys, anys, anys, anys, anys],
        out_specs=[vmem] * 2,
        scratch_shapes=[
            VMEM((2, KEYS, HD), BF16),
            VMEM((2, KEYS + 16, HD), BF16),
            VMEM((SLOTS, NZH, KEYS, HD), BF16),
            VMEM((SLOTS, NZH, KEYS + 16, HD), BF16),
            VMEM((SLOTS, NZH, KEYS, HD), BF16),
            VMEM((SLOTS, NZH, KEYS + 16, HD), BF16),
            VMEM((RING, SEQ, ROWS, HD), BF16),
            VMEM((RING, 1, SEQ), jnp.int32),
            pltpu.SMEM((RING, 1, SEQ), jnp.int32),
            VMEM((RING, SEQ, ROWS, HD), BF16),
            VMEM((RING, 8, 128), F32),
            VMEM((RING, SEQ, ROWS, HD), BF16),
            VMEM((RING, 8, 128), F32),
            VMEM((SEQ, KVH * ROWS, HD), F32),
            VMEM((KVH * ROWS, 128), F32),
            VMEM((1, C, 2 * PER_KV * HD), BF16),
            VMEM((SEQ, KVH, ROWS, HD), BF16),
            VMEM((SEQ, 2, LOC, KVH * HD), BF16),
            VMEM((SEQ, 2, KVH * STEPS, HD), BF16),
            sem((8,)),
            sem((4,)),
        ]
        + [sem((RING - 1,))] * 4
        + [sem((4,))] * 2
        + [sem((3, 2, 4))] * 2
        + [sem((3, 2, 4, 4))] * 2
        + [sem((3, 2, 4, 4))] * 2
        + [sem((RING,))] * 4,
        compiler_params=pltpu.CompilerParams(
            collective_id=0, has_side_effects=True, vmem_limit_bytes=58 * MIB
        ),
        name="attention",
    )(prefix_length, cache_length[0], prompt_q, prompt_kv, q, decode_kv[0], fresh, src)
    prompt_out, out = pl.pallas_call(
        copy_kernel,
        out_shape=(shape(prompt_out.shape, BF16), shape(out.shape, BF16)),
        in_specs=[anys] * 2,
        out_specs=[anys] * 2,
        scratch_shapes=[
            VMEM(prompt_out.shape, BF16),
            VMEM(out.shape, BF16),
            sem((PARTS + 1,)),
            sem((PARTS + 1,)),
        ],
        name="place",
    )(prompt_out, out)
    out = out.reshape(SEQ, HEADS, STEPS, HD).transpose(0, 2, 1, 3)
    return prompt_out, out.reshape(1, SEQ, STEPS, HEADS * HD)


def solution(mesh):
    return jax.shard_map(
        shards,
        mesh=mesh,
        in_specs=(
            P("role", None, "tp"),
            P("role", None, None, "tp"),
            P("role"),
            P("role", "tp", None, None),
            P("role", "tp", None, None, None),
            P("role", "tp", None, None, None),
            P("role", "tp", None),
            P("role", "tp"),
        ),
        out_specs=(P("role", None, "tp"), P("role", "tp", None, None)),
        check_vma=False,
    )
```

```python
import math

import jax
import jax.numpy as jnp
from jax import lax
from jax.experimental import pallas as pl
from jax.experimental.pallas import tpu as pltpu
from jax.sharding import PartitionSpec as P

HEADS = 64
KVH = 8
PER_KV = HEADS // KVH
HD = 128
C = 64
PRE = 128
KEYS = PRE + C
LOC = 16
SEQ = 32
STEPS = 2
ROWS = PER_KV * STEPS
NX, NY, NZH, NC, NZL = 4, 4, 2, 2, 4
RING = NZH * NZL
SLOTS = NC * NX * NY
SCALE = 1.0 / math.sqrt(HD)
NEGATIVE = -1e30
PARTS = 4
LOCAL_KEYS = KVH * (LOC + STEPS)

F32 = jnp.float32
BF16 = jnp.bfloat16
VMEM = pltpu.VMEM
MIB = 1024 * 1024


def position():
    role = lax.axis_index("role")
    z_lo = lax.axis_index("tp")
    core = lax.rem(role, NC)
    z_hi = lax.rem(role // NC, NZH)
    y = lax.rem(role // (NC * NZH), NY)
    x = role // (NC * NZH * NY)
    return x, y, z_hi, core, z_lo


def device(x, y, z_hi, core, z_lo):
    return (((x * NY + y) * NZH + z_hi) * NC + core, z_lo)


def ring_device(x, y, core, ring):
    return device(x, y, ring // NZL, core, lax.rem(ring, NZL))


def ring_head(ring):
    return 2 * lax.rem(ring, NZL) + ring // NZL


def slot_of(x, y, core):
    return (core * NX + x) * NY + y


def nt_dot(a, b):
    return lax.dot_general(a, b, (((1,), (1,)), ((), ())), preferred_element_type=F32)


def dot(a, b):
    return jnp.dot(a, b, preferred_element_type=F32)


def enter(peers):
    barrier = pltpu.get_barrier_semaphore()
    for peer in peers:
        pl.semaphore_signal(barrier, inc=1, device_id=peer, device_id_type=pl.DeviceIdType.MESH)
    pl.semaphore_wait(barrier, len(peers))


def remote(src, dst, send, recv, peer):
    return pltpu.make_async_remote_copy(
        src_ref=src,
        dst_ref=dst,
        send_sem=send,
        recv_sem=recv,
        device_id=peer,
        device_id_type=pl.DeviceIdType.MESH,
    )


def prefill_part(c, plen, prompt_q, blk_a, blk_b, prompt_out):
    position_of = lax.broadcasted_iota(jnp.int32, (C, KEYS), 1)
    own_row = lax.broadcasted_iota(jnp.int32, (C, KEYS), 0)
    usable = (position_of < plen[0]) | ((position_of >= PRE) & (position_of - PRE <= own_row))
    keys = blk_a[c]
    values = blk_b[c, 0:KEYS]
    for g in range(PER_KV):
        columns = slice((c * PER_KV + g) * HD, (c * PER_KV + g + 1) * HD)
        scores = nt_dot(prompt_q[0, :, columns], keys) * SCALE
        scores = jnp.where(usable, scores, NEGATIVE)
        highest = jnp.max(scores, axis=-1, keepdims=True)
        terms = jnp.where(usable, jnp.exp(scores - highest), 0.0)
        total = jnp.sum(terms, axis=-1, keepdims=True)
        weighted = dot(terms.astype(BF16), values)
        prompt_out[0, :, columns] = (weighted / total).astype(BF16)


def local_part(first, last, lengths, q, cache, fresh, acc, stats):
    all_rows = KVH * ROWS
    row = lax.broadcasted_iota(jnp.int32, (all_rows, LOCAL_KEYS), 0)
    col = lax.broadcasted_iota(jnp.int32, (all_rows, LOCAL_KEYS), 1)
    in_cache = col < KVH * LOC
    head = row // ROWS
    cache_ok = in_cache & (col // LOC == head)
    fresh_col = col - KVH * LOC
    fresh_ok = (~in_cache) & (fresh_col // STEPS == head) & (fresh_col % STEPS <= row % STEPS)
    rank = jnp.where(cache_ok, col % LOC, jnp.where(fresh_ok, -1, 2 * LOC))
    lane = lax.broadcasted_iota(jnp.int32, (all_rows, 128), 1)
    group = 2

    def rows_of(s, which):
        return jnp.concatenate(
            [cache[s, which, :, h * HD : (h + 1) * HD] for h in range(KVH)] + [fresh[s, which]],
            axis=0,
        )

    def body(block, table):
        seqs = [block * group + i for i in range(group)]
        usable = [rank < lengths[s] for s in seqs]
        scores = [nt_dot(q[s].reshape(all_rows, HD), rows_of(s, 0)) for s in seqs]
        scores = [jnp.where(u, x * SCALE, NEGATIVE) for u, x in zip(usable, scores)]
        highest = [jnp.max(x, axis=-1, keepdims=True) for x in scores]
        terms = [
            jnp.where(u, jnp.exp(x - h), 0.0) for u, x, h in zip(usable, scores, highest)
        ]
        total = [jnp.sum(x, axis=-1, keepdims=True) for x in terms]
        weighted = [dot(x.astype(BF16), rows_of(s, 1)) for x, s in zip(terms, seqs)]
        for i, s in enumerate(seqs):
            acc[s] = weighted[i]
            table = jnp.where(lane == s, highest[i], table)
            table = jnp.where(lane == s + 64, total[i], table)
        return table

    start = jnp.zeros((all_rows, 128), F32) if first == 0 else stats[...]
    stats[...] = lax.fori_loop(first // group, last // group, body, start)


def remote_part(ring, sources, ka, kb, qg, ro, rs):
    lane = lax.broadcasted_iota(jnp.int32, (ROWS, 128), 1)
    group = 32

    def body(block, table):
        seqs = [block * group + i for i in range(group)]
        places = []
        for s in seqs:
            prompt = sources[ring, 0, s]
            slot = lax.rem(prompt, NC) * (SLOTS // NC) + prompt // (NC * NZH)
            places.append((slot, lax.rem(prompt // NC, NZH)))
        scores = jnp.concatenate(
            [nt_dot(qg[ring, s], ka[slot, half]) for s, (slot, half) in zip(seqs, places)], axis=0
        )
        scores = scores * SCALE
        bias = jnp.concatenate([kb[slot, half, KEYS:] for slot, half in places], axis=0)
        prefix = scores[:, 0:PRE] + bias.astype(F32)
        stretch = scores[:, PRE:]
        highest = jnp.maximum(
            jnp.max(prefix, axis=-1, keepdims=True), jnp.max(stretch, axis=-1, keepdims=True)
        )
        terms = jnp.concatenate([jnp.exp(prefix - highest), jnp.exp(stretch - highest)], axis=1)
        total = jnp.sum(terms, axis=-1, keepdims=True)
        weights = terms.astype(BF16)
        for i, (s, (slot, half)) in enumerate(zip(seqs, places)):
            rows = slice(i * ROWS, (i + 1) * ROWS)
            weighted = dot(weights[rows], kb[slot, half, 0:KEYS])
            ro[ring, s] = (weighted / total[rows]).astype(BF16)
            table = jnp.where(lane == s, highest[rows], table)
            table = jnp.where(lane == s + 64, total[rows], table)
        return table

    table = lax.fori_loop(0, SEQ // group, body, jnp.zeros((ROWS, 128), F32))
    rs[ring] = table[0:8] + pltpu.roll(table[8:16], SEQ, 1)


def merge_part(ring, bo, bs, acc, stats, out):
    head = ring_head(ring)
    packed = bs[ring]
    far = jnp.concatenate([packed, pltpu.roll(packed, 128 - SEQ, 1)], axis=0)
    rows = pl.ds(pl.multiple_of(head * ROWS, ROWS), ROWS)
    near = stats[rows]
    far_sum = pltpu.roll(far, 64, 1)
    near_sum = pltpu.roll(near, 64, 1)
    peak = jnp.maximum(far, near)
    near_scale = jnp.exp(near - peak)
    far_share = far_sum * jnp.exp(far - peak)
    whole = far_share + near_sum * near_scale
    far_weight = far_share / whole
    near_weight = near_scale / whole
    for s in range(SEQ):
        merged = (
            far_weight[:, s : s + 1] * bo[ring, s].astype(F32)
            + near_weight[:, s : s + 1] * acc[s, rows]
        )
        out[s, head] = merged.astype(BF16)


def kernel(
    plen, lengths, prompt_q_hbm, kv, q, cache_hbm, fresh_hbm, src, prompt_out, out,
    blk_a, blk_b, ka, kb, ka2, kb2, qg, srcg, sources, ro, rs, bo, bs, acc, stats,
    prompt_q, q_own, cache, fresh, load, local,
    send_q, recv_q, send_s, recv_s, send_f, recv_f, send_1, recv_1, send_2, recv_2, send_c, recv_c,
    send_o, recv_o, send_t, recv_t,
):
    x, y, zh, core, zl = position()
    ring = zh * NZL + zl
    opposite = lax.rem(ring + RING // 2, RING)
    sibling = device(x, y, zh, 1 - core, zl)
    ring_peers = [ring_device(x, y, core, lax.rem(ring + d, RING)) for d in range(1, RING)]
    x_peers = [device(lax.rem(x + d, NX), y, zh, core, zl) for d in range(1, NX)]
    y_peers = [device(x, lax.rem(y + d, NY), zh, core, zl) for d in range(1, NY)]

    blocks = []
    for half in range(2):
        columns = slice(half * HD, (half + 1) * HD)
        blocks.append(
            pltpu.make_async_copy(kv.at[0, 0, :, columns], blk_a.at[half], load.at[half])
        )
        blocks.append(
            pltpu.make_async_copy(
                kv.at[0, 1, :, columns], blk_b.at[half, 0:KEYS], load.at[2 + half]
            )
        )
    loads = [
        pltpu.make_async_copy(prompt_q_hbm, prompt_q, load.at[4]),
        pltpu.make_async_copy(q, q_own, load.at[5]),
        pltpu.make_async_copy(cache_hbm, cache, load.at[6]),
        pltpu.make_async_copy(fresh_hbm, fresh, load.at[7]),
    ]
    local_copies = [
        pltpu.make_async_copy(q.at[:, ring_head(ring)], qg.at[ring], local.at[0]),
        pltpu.make_async_copy(q.at[:, ring_head(opposite)], qg.at[opposite], local.at[1]),
        pltpu.make_async_copy(src, srcg.at[ring], local.at[2]),
    ]
    for copy in blocks + loads + local_copies:
        copy.start()
    row_bias = jnp.where(
        lax.broadcasted_iota(jnp.int32, (16, PRE), 1) < plen[0], 0.0, NEGATIVE
    ).astype(BF16)
    for half in range(2):
        blk_b[half, KEYS:] = row_bias
    for copy in blocks:
        copy.wait()
    mine = slot_of(x, y, core)
    ka[mine, zh] = blk_a[zh]
    kb[mine, zh] = blk_b[zh]
    ka2[mine, zh] = blk_a[1 - zh]
    kb2[mine, zh] = blk_b[1 - zh]
    enter(ring_peers + x_peers + y_peers + [sibling])

    antipode = ring_peers[RING // 2 - 1]
    far_copies = [
        remote(blk.at[head], dst.at[mine, zh], send_f.at[i], recv_f.at[i], antipode)
        for i, (blk, dst, head) in enumerate(
            ((blk_a, ka, 1 - zh), (blk_b, kb, 1 - zh), (blk_a, ka2, zh), (blk_b, kb2, zh))
        )
    ]
    for copy in far_copies[:2]:
        copy.start()

    def slot_at(path, first, second):
        dx, dy = (first, second) if path == 0 else (second, first)
        return slot_of(lax.rem(x + NX - dx, NX), lax.rem(y + NY - dy, NY), core)

    def along(path, phase, d):
        return (x_peers if (path + phase) % 2 == 0 else y_peers)[d - 1]

    streams = (
        (lambda slot: (ka.at[slot, zh], kb.at[slot, zh])),
        (lambda slot: (ka.at[slot, 1 - zh], kb.at[slot, 1 - zh])),
        (lambda slot: (ka2.at[slot], kb2.at[slot])),
    )
    pieces = ((), (), ((0, 1), (1, 3)))

    def part(stream, path, slot, piece):
        ref = streams[stream](slot)[path]
        return ref if piece is None else ref.at[piece]

    def first_copies(stream, path, way):
        if way != 2 or not pieces[stream]:
            ref = part(stream, path, mine, None)
            return [
                remote(
                    ref, ref, send_1.at[stream, path, way], recv_1.at[stream, path, way],
                    along(path, 0, way),
                )
            ]
        copies = []
        for piece, to in pieces[stream]:
            ref = part(stream, path, slot_at(path, to, 0), piece)
            i = 0 if to == 1 else 2
            copies.append(
                remote(
                    ref, ref, send_1.at[stream, path, i], recv_1.at[stream, path, i],
                    along(path, 0, to),
                )
            )
        return copies

    def second_copies(stream, path, d, way):
        if way != 2 or not pieces[stream]:
            ref = part(stream, path, slot_at(path, d, 0), None)
            return [
                remote(
                    ref, ref, send_2.at[stream, path, d, way], recv_2.at[stream, path, d, way],
                    along(path, 1, way),
                )
            ]
        copies = []
        for piece, to in pieces[stream]:
            ref = part(stream, path, slot_at(path, d, to), piece)
            i = 0 if to == 1 else 2
            copies.append(
                remote(
                    ref, ref, send_2.at[stream, path, d, i], recv_2.at[stream, path, d, i],
                    along(path, 1, to),
                )
            )
        return copies

    def side_copies(stream, path, d, e):
        ref = part(stream, path, slot_at(path, d, e), None)
        return [
            remote(
                ref, ref, send_c.at[stream, path, d, e], recv_c.at[stream, path, d, e], sibling
            )
        ]

    def start(copies):
        for copy in copies:
            copy.start()

    def arrived(copies):
        for copy in copies:
            copy.wait_recv()

    def gone(copies):
        for copy in copies:
            copy.wait_send()

    def begin(stream):
        for path in range(2):
            start(first_copies(stream, path, 1))
            start(first_copies(stream, path, 3))
            if not pieces[stream]:
                start(first_copies(stream, path, 2))

    def go_on(stream):
        if not pieces[stream]:
            return
        for path in range(2):
            for piece, to in pieces[stream]:
                arrived(first_copies(stream, path, to))
            start(first_copies(stream, path, 2))

    def spread(stream, d):
        passed = [to for piece, to in pieces[stream]]
        for path in range(2):
            if d > 0 and d not in passed:
                arrived(first_copies(stream, path, d))
            start(second_copies(stream, path, d, 1))
            start(second_copies(stream, path, d, 3))
            if not pieces[stream]:
                start(second_copies(stream, path, d, 2))
            start(side_copies(stream, path, d, 0))

    def go_on_second(stream, d):
        if not pieces[stream]:
            return
        for path in range(2):
            for piece, to in pieces[stream]:
                arrived(second_copies(stream, path, d, to))
            start(second_copies(stream, path, d, 2))
            for piece, to in pieces[stream]:
                start(side_copies(stream, path, d, to))

    def finish(stream, d):
        passed = [to for piece, to in pieces[stream]]
        for path in range(2):
            for way in (1, 3, 2):
                if way not in passed:
                    arrived(second_copies(stream, path, d, way))
                    start(side_copies(stream, path, d, way))

    def sides(stream):
        return [
            copy
            for path in range(2)
            for d in range(4)
            for e in range(4)
            for copy in side_copies(stream, path, d, e)
        ]

    def spreading(stream):
        copies = []
        for path in range(2):
            for way in (1, 3, 2):
                copies += first_copies(stream, path, way)
                for d in range(4):
                    copies += second_copies(stream, path, d, way)
        return copies

    def local_rows(first, last):
        local_part(first, last, lengths, q_own, cache, fresh, acc, stats)

    begin(0)
    spread(0, 0)
    q_copies = []
    src_copies = []
    for d in (3, 5, 2, 6, 1, 7):
        other = lax.rem(ring + d, RING)
        src_copies.append(
            remote(src, srcg.at[ring], send_s.at[d - 1], recv_s.at[d - 1], ring_peers[d - 1])
        )
        q_copies.append(
            remote(
                q.at[:, ring_head(other)],
                qg.at[ring],
                send_q.at[d - 1],
                recv_q.at[d - 1],
                ring_peers[d - 1],
            )
        )
    start(far_copies[2:])
    start(src_copies + q_copies)
    go_on(0)
    spread(0, 1)
    spread(0, 3)
    loads[0].wait()
    prefill_part(0, plen, prompt_q, blk_a, blk_b, prompt_out)
    spread(0, 2)
    arrived(far_copies[:2])
    begin(1)
    spread(1, 0)
    go_on_second(0, 0)
    for copy in loads[1:]:
        copy.wait()
    prefill_part(1, plen, prompt_q, blk_a, blk_b, prompt_out)
    go_on(1)
    spread(1, 1)
    spread(1, 3)
    go_on_second(0, 1)
    go_on_second(0, 3)
    spread(1, 2)
    arrived(far_copies[2:])
    begin(2)
    spread(2, 0)
    local_rows(0, 4)
    go_on_second(1, 0)
    go_on_second(0, 2)
    local_rows(4, 8)
    go_on_second(1, 1)
    go_on_second(1, 3)
    local_rows(8, 12)
    go_on_second(1, 2)
    local_rows(12, 16)
    for d in (0, 1, 3, 2):
        finish(0, d)
    local_rows(16, 24)
    arrived(src_copies)
    for copy in local_copies:
        copy.wait()
    srcg[opposite] = srcg[ring]
    place = pltpu.make_async_copy(srcg, sources, local.at[3])
    place.start()
    local_rows(24, 32)
    place.wait()
    for d in (0, 1, 3, 2):
        finish(1, d)
    go_on(2)
    spread(2, 1)
    spread(2, 3)
    arrived(q_copies)
    arrived(sides(0) + sides(1))

    def answers(d):
        other = lax.rem(ring + d, RING)
        return [
            remote(
                ro.at[other], bo.at[ring], send_o.at[d], recv_o.at[d],
                ring_device(x, y, core, other),
            ),
            remote(
                rs.at[other], bs.at[ring], send_t.at[d], recv_t.at[d],
                ring_device(x, y, core, other),
            ),
        ]

    def distance(k):
        return RING // 2 + (2 * lax.rem(k, 2) - 1) * (1 + k // 2)

    def answer(k, carry):
        d = distance(k)
        remote_part(lax.rem(ring + d, RING), sources, ka, kb, qg, ro, rs)

        @pl.when(k < RING - 2)
        def _():
            start(answers(d))

        @pl.when(k == 0)
        def _():
            spread(2, 2)

        @pl.when(k == 1)
        def _():
            go_on_second(2, 0)

        @pl.when(k == 3)
        def _():
            go_on_second(2, 1)
            go_on_second(2, 3)

        @pl.when(k == 4)
        def _():
            go_on_second(2, 2)

        return carry

    def merge(k, carry):
        d = distance(k)
        for copy in answers(d):
            copy.wait()
        merge_part(lax.rem(ring + RING - d, RING), bo, bs, acc, stats, out)
        return carry

    lax.fori_loop(0, RING - 1, answer, 0)
    for d in (0, 1, 3, 2):
        finish(2, d)
    lax.fori_loop(0, 2, merge, 0)
    arrived(sides(2))
    remote_part(opposite, sources, ka2, kb2, qg, ro, rs)
    for place_at in (ring, opposite):
        bo[place_at] = ro[place_at]
        bs[place_at] = rs[place_at]
        merge_part(place_at, bo, bs, acc, stats, out)
    lax.fori_loop(2, RING - 2, merge, 0)
    gone(q_copies + src_copies + far_copies)
    for stream in range(3):
        gone(spreading(stream) + sides(stream))


def copy_kernel(a, b, out_a, out_b, stage_a, stage_b, sem_in, sem_out):
    loads = [pltpu.make_async_copy(a, stage_a, sem_in.at[PARTS])]
    stores = [pltpu.make_async_copy(stage_a, out_a, sem_out.at[PARTS])]
    for i in range(PARTS):
        rows = pl.ds(i * (SEQ // PARTS), SEQ // PARTS)
        loads.append(pltpu.make_async_copy(b.at[rows], stage_b.at[rows], sem_in.at[i]))
        stores.append(pltpu.make_async_copy(stage_b.at[rows], out_b.at[rows], sem_out.at[i]))
    for copy in loads:
        copy.start()
    for load, store in zip(loads, stores):
        load.wait()
        store.start()
    for copy in stores:
        copy.wait()


def shards(
    prompt_q, prompt_kv, prefix_length, decode_q, decode_kv, fresh_kv, source_prompt, cache_length
):
    q = decode_q[0].reshape(SEQ, STEPS, HEADS, HD).transpose(0, 2, 1, 3)
    q = q.reshape(SEQ, KVH, ROWS, HD)
    fresh = fresh_kv[0].reshape(SEQ, 2, STEPS, KVH, HD).transpose(0, 1, 3, 2, 4)
    fresh = fresh.reshape(SEQ, 2, KVH * STEPS, HD)
    src = source_prompt[0, :, 0][None, :]
    vmem = pl.BlockSpec(memory_space=VMEM)
    smem = pl.BlockSpec(memory_space=pltpu.SMEM)
    anys = pl.BlockSpec(memory_space=pl.ANY)
    shape = jax.ShapeDtypeStruct
    sem = pltpu.SemaphoreType.DMA
    prompt_out, out = pl.pallas_call(
        kernel,
        out_shape=(
            shape((1, C, 2 * PER_KV * HD), BF16),
            shape((SEQ, KVH, ROWS, HD), BF16),
        ),
        in_specs=[smem, smem, anys, anys, anys, anys, anys, anys],
        out_specs=[vmem] * 2,
        scratch_shapes=[
            VMEM((2, KEYS, HD), BF16),
            VMEM((2, KEYS + 16, HD), BF16),
            VMEM((SLOTS, NZH, KEYS, HD), BF16),
            VMEM((SLOTS, NZH, KEYS + 16, HD), BF16),
            VMEM((SLOTS, NZH, KEYS, HD), BF16),
            VMEM((SLOTS, NZH, KEYS + 16, HD), BF16),
            VMEM((RING, SEQ, ROWS, HD), BF16),
            VMEM((RING, 1, SEQ), jnp.int32),
            pltpu.SMEM((RING, 1, SEQ), jnp.int32),
            VMEM((RING, SEQ, ROWS, HD), BF16),
            VMEM((RING, 8, 128), F32),
            VMEM((RING, SEQ, ROWS, HD), BF16),
            VMEM((RING, 8, 128), F32),
            VMEM((SEQ, KVH * ROWS, HD), F32),
            VMEM((KVH * ROWS, 128), F32),
            VMEM((1, C, 2 * PER_KV * HD), BF16),
            VMEM((SEQ, KVH, ROWS, HD), BF16),
            VMEM((SEQ, 2, LOC, KVH * HD), BF16),
            VMEM((SEQ, 2, KVH * STEPS, HD), BF16),
            sem((8,)),
            sem((4,)),
        ]
        + [sem((RING - 1,))] * 4
        + [sem((4,))] * 2
        + [sem((3, 2, 4))] * 2
        + [sem((3, 2, 4, 4))] * 2
        + [sem((3, 2, 4, 4))] * 2
        + [sem((RING,))] * 4,
        compiler_params=pltpu.CompilerParams(
            collective_id=0, has_side_effects=True, vmem_limit_bytes=58 * MIB
        ),
        name="attention",
    )(prefix_length, cache_length[0], prompt_q, prompt_kv, q, decode_kv[0], fresh, src)
    prompt_out, out = pl.pallas_call(
        copy_kernel,
        out_shape=(shape(prompt_out.shape, BF16), shape(out.shape, BF16)),
        in_specs=[anys] * 2,
        out_specs=[anys] * 2,
        scratch_shapes=[
            VMEM(prompt_out.shape, BF16),
            VMEM(out.shape, BF16),
            sem((PARTS + 1,)),
            sem((PARTS + 1,)),
        ],
        name="place",
    )(prompt_out, out)
    out = out.reshape(SEQ, HEADS, STEPS, HD).transpose(0, 2, 1, 3)
    return prompt_out, out.reshape(1, SEQ, STEPS, HEADS * HD)


def solution(mesh):
    return jax.shard_map(
        shards,
        mesh=mesh,
        in_specs=(
            P("role", None, "tp"),
            P("role", None, None, "tp"),
            P("role"),
            P("role", "tp", None, None),
            P("role", "tp", None, None, None),
            P("role", "tp", None, None, None),
            P("role", "tp", None),
            P("role", "tp"),
        ),
        out_specs=(P("role", None, "tp"), P("role", "tp", None, None)),
        check_vma=False,
    )
```

```python
import math

import jax
import jax.numpy as jnp
from jax import lax
from jax.experimental import pallas as pl
from jax.experimental.pallas import tpu as pltpu
from jax.sharding import PartitionSpec as P

HEADS = 64
KVH = 8
PER_KV = HEADS // KVH
HD = 128
C = 64
PRE = 128
KEYS = PRE + C
LOC = 16
SEQ = 32
STEPS = 2
ROWS = PER_KV * STEPS
NX, NY, NZH, NC, NZL = 4, 4, 2, 2, 4
RING = NZH * NZL
SLOTS = NC * NX * NY
SCALE = 1.0 / math.sqrt(HD)
NEGATIVE = -1e30
PARTS = 4
LOCAL_KEYS = KVH * (LOC + STEPS)

F32 = jnp.float32
BF16 = jnp.bfloat16
VMEM = pltpu.VMEM
MIB = 1024 * 1024


def position():
    role = lax.axis_index("role")
    z_lo = lax.axis_index("tp")
    core = lax.rem(role, NC)
    z_hi = lax.rem(role // NC, NZH)
    y = lax.rem(role // (NC * NZH), NY)
    x = role // (NC * NZH * NY)
    return x, y, z_hi, core, z_lo


def device(x, y, z_hi, core, z_lo):
    return (((x * NY + y) * NZH + z_hi) * NC + core, z_lo)


def ring_device(x, y, core, ring):
    return device(x, y, ring // NZL, core, lax.rem(ring, NZL))


def ring_head(ring):
    return 2 * lax.rem(ring, NZL) + ring // NZL


def slot_of(x, y, core):
    return (core * NX + x) * NY + y


def nt_dot(a, b):
    return lax.dot_general(a, b, (((1,), (1,)), ((), ())), preferred_element_type=F32)


def dot(a, b):
    return jnp.dot(a, b, preferred_element_type=F32)


def enter(peers):
    barrier = pltpu.get_barrier_semaphore()
    for peer in peers:
        pl.semaphore_signal(barrier, inc=1, device_id=peer, device_id_type=pl.DeviceIdType.MESH)
    pl.semaphore_wait(barrier, len(peers))


def remote(src, dst, send, recv, peer):
    return pltpu.make_async_remote_copy(
        src_ref=src,
        dst_ref=dst,
        send_sem=send,
        recv_sem=recv,
        device_id=peer,
        device_id_type=pl.DeviceIdType.MESH,
    )


def prefill_part(c, plen, prompt_q, blk_a, blk_b, prompt_out):
    position_of = lax.broadcasted_iota(jnp.int32, (C, KEYS), 1)
    own_row = lax.broadcasted_iota(jnp.int32, (C, KEYS), 0)
    usable = (position_of < plen[0]) | ((position_of >= PRE) & (position_of - PRE <= own_row))
    keys = blk_a[c]
    values = blk_b[c, 0:KEYS]
    for g in range(PER_KV):
        columns = slice((c * PER_KV + g) * HD, (c * PER_KV + g + 1) * HD)
        scores = nt_dot(prompt_q[0, :, columns], keys) * SCALE
        scores = jnp.where(usable, scores, NEGATIVE)
        highest = jnp.max(scores, axis=-1, keepdims=True)
        terms = jnp.where(usable, jnp.exp(scores - highest), 0.0)
        total = jnp.sum(terms, axis=-1, keepdims=True)
        weighted = dot(terms.astype(BF16), values)
        prompt_out[0, :, columns] = (weighted / total).astype(BF16)


def local_part(first, last, lengths, q, cache, fresh, acc, stats):
    all_rows = KVH * ROWS
    row = lax.broadcasted_iota(jnp.int32, (all_rows, LOCAL_KEYS), 0)
    col = lax.broadcasted_iota(jnp.int32, (all_rows, LOCAL_KEYS), 1)
    in_cache = col < KVH * LOC
    head = row // ROWS
    cache_ok = in_cache & (col // LOC == head)
    fresh_col = col - KVH * LOC
    fresh_ok = (~in_cache) & (fresh_col // STEPS == head) & (fresh_col % STEPS <= row % STEPS)
    rank = jnp.where(cache_ok, col % LOC, jnp.where(fresh_ok, -1, 2 * LOC))
    lane = lax.broadcasted_iota(jnp.int32, (all_rows, 128), 1)
    group = 2

    def rows_of(s, which):
        return jnp.concatenate(
            [cache[s, which, :, h * HD : (h + 1) * HD] for h in range(KVH)] + [fresh[s, which]],
            axis=0,
        )

    def body(block, table):
        seqs = [block * group + i for i in range(group)]
        usable = [rank < lengths[s] for s in seqs]
        scores = [nt_dot(q[s].reshape(all_rows, HD), rows_of(s, 0)) for s in seqs]
        scores = [jnp.where(u, x * SCALE, NEGATIVE) for u, x in zip(usable, scores)]
        highest = [jnp.max(x, axis=-1, keepdims=True) for x in scores]
        terms = [
            jnp.where(u, jnp.exp(x - h), 0.0) for u, x, h in zip(usable, scores, highest)
        ]
        total = [jnp.sum(x, axis=-1, keepdims=True) for x in terms]
        weighted = [dot(x.astype(BF16), rows_of(s, 1)) for x, s in zip(terms, seqs)]
        for i, s in enumerate(seqs):
            acc[s] = weighted[i]
            table = jnp.where(lane == s, highest[i], table)
            table = jnp.where(lane == s + 64, total[i], table)
        return table

    start = jnp.zeros((all_rows, 128), F32) if first == 0 else stats[...]
    stats[...] = lax.fori_loop(first // group, last // group, body, start)


def remote_part(ring, sources, ka, kb, qg, ro, rs):
    lane = lax.broadcasted_iota(jnp.int32, (ROWS, 128), 1)
    group = 32

    def body(block, table):
        seqs = [block * group + i for i in range(group)]
        places = []
        for s in seqs:
            prompt = sources[ring, 0, s]
            slot = lax.rem(prompt, NC) * (SLOTS // NC) + prompt // (NC * NZH)
            places.append((slot, lax.rem(prompt // NC, NZH)))
        scores = jnp.concatenate(
            [nt_dot(qg[ring, s], ka[slot, half]) for s, (slot, half) in zip(seqs, places)], axis=0
        )
        scores = scores * SCALE
        bias = jnp.concatenate([kb[slot, half, KEYS:] for slot, half in places], axis=0)
        prefix = scores[:, 0:PRE] + bias.astype(F32)
        stretch = scores[:, PRE:]
        highest = jnp.maximum(
            jnp.max(prefix, axis=-1, keepdims=True), jnp.max(stretch, axis=-1, keepdims=True)
        )
        terms = jnp.concatenate([jnp.exp(prefix - highest), jnp.exp(stretch - highest)], axis=1)
        total = jnp.sum(terms, axis=-1, keepdims=True)
        weights = terms.astype(BF16)
        for i, (s, (slot, half)) in enumerate(zip(seqs, places)):
            rows = slice(i * ROWS, (i + 1) * ROWS)
            weighted = dot(weights[rows], kb[slot, half, 0:KEYS])
            ro[ring, s] = (weighted / total[rows]).astype(BF16)
            table = jnp.where(lane == s, highest[rows], table)
            table = jnp.where(lane == s + 64, total[rows], table)
        return table

    table = lax.fori_loop(0, SEQ // group, body, jnp.zeros((ROWS, 128), F32))
    rs[ring] = table[0:8] + pltpu.roll(table[8:16], SEQ, 1)


def merge_part(ring, bo, bs, acc, stats, out):
    head = ring_head(ring)
    packed = bs[ring]
    far = jnp.concatenate([packed, pltpu.roll(packed, 128 - SEQ, 1)], axis=0)
    rows = pl.ds(pl.multiple_of(head * ROWS, ROWS), ROWS)
    near = stats[rows]
    far_sum = pltpu.roll(far, 64, 1)
    near_sum = pltpu.roll(near, 64, 1)
    peak = jnp.maximum(far, near)
    near_scale = jnp.exp(near - peak)
    far_share = far_sum * jnp.exp(far - peak)
    whole = far_share + near_sum * near_scale
    far_weight = far_share / whole
    near_weight = near_scale / whole
    for s in range(SEQ):
        merged = (
            far_weight[:, s : s + 1] * bo[ring, s].astype(F32)
            + near_weight[:, s : s + 1] * acc[s, rows]
        )
        out[s, head] = merged.astype(BF16)


def kernel(
    plen, lengths, prompt_q_hbm, kv, q, cache_hbm, fresh_hbm, src, prompt_out, out,
    blk_a, blk_b, ka, kb, ka2, kb2, qg, srcg, sources, ro, rs, bo, bs, acc, stats,
    prompt_q, q_own, cache, fresh, load, local,
    send_q, recv_q, send_s, recv_s, send_f, recv_f, send_1, recv_1, send_2, recv_2, send_c, recv_c,
    send_o, recv_o, send_t, recv_t,
):
    x, y, zh, core, zl = position()
    ring = zh * NZL + zl
    opposite = lax.rem(ring + RING // 2, RING)
    sibling = device(x, y, zh, 1 - core, zl)
    ring_peers = [ring_device(x, y, core, lax.rem(ring + d, RING)) for d in range(1, RING)]
    x_peers = [device(lax.rem(x + d, NX), y, zh, core, zl) for d in range(1, NX)]
    y_peers = [device(x, lax.rem(y + d, NY), zh, core, zl) for d in range(1, NY)]

    blocks = []
    for half in range(2):
        columns = slice(half * HD, (half + 1) * HD)
        blocks.append(
            pltpu.make_async_copy(kv.at[0, 0, :, columns], blk_a.at[half], load.at[half])
        )
        blocks.append(
            pltpu.make_async_copy(
                kv.at[0, 1, :, columns], blk_b.at[half, 0:KEYS], load.at[2 + half]
            )
        )
    loads = [
        pltpu.make_async_copy(prompt_q_hbm, prompt_q, load.at[4]),
        pltpu.make_async_copy(q, q_own, load.at[5]),
        pltpu.make_async_copy(cache_hbm, cache, load.at[6]),
        pltpu.make_async_copy(fresh_hbm, fresh, load.at[7]),
    ]
    local_copies = [
        pltpu.make_async_copy(q.at[:, ring_head(ring)], qg.at[ring], local.at[0]),
        pltpu.make_async_copy(q.at[:, ring_head(opposite)], qg.at[opposite], local.at[1]),
        pltpu.make_async_copy(src, srcg.at[ring], local.at[2]),
    ]
    for copy in blocks + loads + local_copies:
        copy.start()
    row_bias = jnp.where(
        lax.broadcasted_iota(jnp.int32, (16, PRE), 1) < plen[0], 0.0, NEGATIVE
    ).astype(BF16)
    for half in range(2):
        blk_b[half, KEYS:] = row_bias
    for copy in blocks:
        copy.wait()
    mine = slot_of(x, y, core)
    ka[mine, zh] = blk_a[zh]
    kb[mine, zh] = blk_b[zh]
    ka2[mine, zh] = blk_a[1 - zh]
    kb2[mine, zh] = blk_b[1 - zh]
    enter(ring_peers + x_peers + y_peers + [sibling])

    antipode = ring_peers[RING // 2 - 1]
    far_copies = [
        remote(blk.at[head], dst.at[mine, zh], send_f.at[i], recv_f.at[i], antipode)
        for i, (blk, dst, head) in enumerate(
            ((blk_a, ka, 1 - zh), (blk_b, kb, 1 - zh), (blk_a, ka2, zh), (blk_b, kb2, zh))
        )
    ]
    for copy in far_copies[:2]:
        copy.start()

    def slot_at(path, first, second):
        dx, dy = (first, second) if path == 0 else (second, first)
        return slot_of(lax.rem(x + NX - dx, NX), lax.rem(y + NY - dy, NY), core)

    def along(path, phase, d):
        return (x_peers if (path + phase) % 2 == 0 else y_peers)[d - 1]

    streams = (
        (lambda slot: (ka.at[slot, zh], kb.at[slot, zh])),
        (lambda slot: (ka.at[slot, 1 - zh], kb.at[slot, 1 - zh])),
        (lambda slot: (ka2.at[slot], kb2.at[slot])),
    )
    pieces = ((), (), ((0, 1), (1, 3)))

    def part(stream, path, slot, piece):
        ref = streams[stream](slot)[path]
        return ref if piece is None else ref.at[piece]

    def first_copies(stream, path, way):
        if way != 2 or not pieces[stream]:
            ref = part(stream, path, mine, None)
            return [
                remote(
                    ref, ref, send_1.at[stream, path, way], recv_1.at[stream, path, way],
                    along(path, 0, way),
                )
            ]
        copies = []
        for piece, to in pieces[stream]:
            ref = part(stream, path, slot_at(path, to, 0), piece)
            i = 0 if to == 1 else 2
            copies.append(
                remote(
                    ref, ref, send_1.at[stream, path, i], recv_1.at[stream, path, i],
                    along(path, 0, to),
                )
            )
        return copies

    def second_copies(stream, path, d, way):
        if way != 2 or not pieces[stream]:
            ref = part(stream, path, slot_at(path, d, 0), None)
            return [
                remote(
                    ref, ref, send_2.at[stream, path, d, way], recv_2.at[stream, path, d, way],
                    along(path, 1, way),
                )
            ]
        copies = []
        for piece, to in pieces[stream]:
            ref = part(stream, path, slot_at(path, d, to), piece)
            i = 0 if to == 1 else 2
            copies.append(
                remote(
                    ref, ref, send_2.at[stream, path, d, i], recv_2.at[stream, path, d, i],
                    along(path, 1, to),
                )
            )
        return copies

    def side_copies(stream, path, d, e):
        ref = part(stream, path, slot_at(path, d, e), None)
        return [
            remote(
                ref, ref, send_c.at[stream, path, d, e], recv_c.at[stream, path, d, e], sibling
            )
        ]

    def start(copies):
        for copy in copies:
            copy.start()

    def arrived(copies):
        for copy in copies:
            copy.wait_recv()

    def gone(copies):
        for copy in copies:
            copy.wait_send()

    def begin(stream):
        for path in range(2):
            start(first_copies(stream, path, 1))
            start(first_copies(stream, path, 3))
            if not pieces[stream]:
                start(first_copies(stream, path, 2))

    def go_on(stream):
        if not pieces[stream]:
            return
        for path in range(2):
            for piece, to in pieces[stream]:
                arrived(first_copies(stream, path, to))
            start(first_copies(stream, path, 2))

    def spread(stream, d):
        passed = [to for piece, to in pieces[stream]]
        for path in range(2):
            if d > 0 and d not in passed:
                arrived(first_copies(stream, path, d))
            start(second_copies(stream, path, d, 1))
            start(second_copies(stream, path, d, 3))
            if not pieces[stream]:
                start(second_copies(stream, path, d, 2))
            start(side_copies(stream, path, d, 0))

    def go_on_second(stream, d):
        if not pieces[stream]:
            return
        for path in range(2):
            for piece, to in pieces[stream]:
                arrived(second_copies(stream, path, d, to))
            start(second_copies(stream, path, d, 2))
            for piece, to in pieces[stream]:
                start(side_copies(stream, path, d, to))

    def finish(stream, d):
        passed = [to for piece, to in pieces[stream]]
        for path in range(2):
            for way in (1, 3, 2):
                if way not in passed:
                    arrived(second_copies(stream, path, d, way))
                    start(side_copies(stream, path, d, way))

    def sides(stream):
        return [
            copy
            for path in range(2)
            for d in range(4)
            for e in range(4)
            for copy in side_copies(stream, path, d, e)
        ]

    def spreading(stream):
        copies = []
        for path in range(2):
            for way in (1, 3, 2):
                copies += first_copies(stream, path, way)
                for d in range(4):
                    copies += second_copies(stream, path, d, way)
        return copies

    def local_rows(first, last):
        local_part(first, last, lengths, q_own, cache, fresh, acc, stats)

    begin(0)
    spread(0, 0)
    q_copies = []
    src_copies = []
    for d in (3, 5, 2, 6, 1, 7):
        other = lax.rem(ring + d, RING)
        src_copies.append(
            remote(src, srcg.at[ring], send_s.at[d - 1], recv_s.at[d - 1], ring_peers[d - 1])
        )
        q_copies.append(
            remote(
                q.at[:, ring_head(other)],
                qg.at[ring],
                send_q.at[d - 1],
                recv_q.at[d - 1],
                ring_peers[d - 1],
            )
        )
    start(far_copies[2:])
    start(src_copies + q_copies)
    go_on(0)
    spread(0, 1)
    spread(0, 3)
    loads[0].wait()
    prefill_part(0, plen, prompt_q, blk_a, blk_b, prompt_out)
    spread(0, 2)
    arrived(far_copies[:2])
    begin(1)
    spread(1, 0)
    go_on_second(0, 0)
    for copy in loads[1:]:
        copy.wait()
    prefill_part(1, plen, prompt_q, blk_a, blk_b, prompt_out)
    go_on(1)
    spread(1, 1)
    spread(1, 3)
    go_on_second(0, 1)
    go_on_second(0, 3)
    spread(1, 2)
    arrived(far_copies[2:])
    begin(2)
    spread(2, 0)
    local_rows(0, 4)
    go_on_second(1, 0)
    go_on_second(0, 2)
    local_rows(4, 8)
    go_on_second(1, 1)
    go_on_second(1, 3)
    local_rows(8, 12)
    go_on_second(1, 2)
    local_rows(12, 16)
    for d in (0, 1, 3, 2):
        finish(0, d)
    local_rows(16, 24)
    arrived(src_copies)
    for copy in local_copies:
        copy.wait()
    srcg[opposite] = srcg[ring]
    place = pltpu.make_async_copy(srcg, sources, local.at[3])
    place.start()
    local_rows(24, 32)
    place.wait()
    for d in (0, 1, 3, 2):
        finish(1, d)
    go_on(2)
    spread(2, 1)
    spread(2, 3)
    arrived(q_copies)
    arrived(sides(0) + sides(1))

    def answers(d):
        other = lax.rem(ring + d, RING)
        return [
            remote(
                ro.at[other], bo.at[ring], send_o.at[d], recv_o.at[d],
                ring_device(x, y, core, other),
            ),
            remote(
                rs.at[other], bs.at[ring], send_t.at[d], recv_t.at[d],
                ring_device(x, y, core, other),
            ),
        ]

    def distance(k):
        return RING // 2 + (2 * lax.rem(k, 2) - 1) * (1 + k // 2)

    def answer(k, carry):
        d = distance(k)
        remote_part(lax.rem(ring + d, RING), sources, ka, kb, qg, ro, rs)

        @pl.when(k < RING - 2)
        def _():
            start(answers(d))

        @pl.when(k == 0)
        def _():
            spread(2, 2)

        @pl.when(k == 1)
        def _():
            go_on_second(2, 0)

        @pl.when(k == 3)
        def _():
            go_on_second(2, 1)
            go_on_second(2, 3)

        @pl.when(k == 4)
        def _():
            go_on_second(2, 2)

        return carry

    def merge(k, carry):
        d = distance(k)
        for copy in answers(d):
            copy.wait()
        merge_part(lax.rem(ring + RING - d, RING), bo, bs, acc, stats, out)
        return carry

    lax.fori_loop(0, RING - 1, answer, 0)
    for d in (0, 1, 3, 2):
        finish(2, d)
    bo[ring] = ro[ring]
    bs[ring] = rs[ring]
    merge_part(ring, bo, bs, acc, stats, out)
    lax.fori_loop(0, 2, merge, 0)
    arrived(sides(2))
    remote_part(opposite, sources, ka2, kb2, qg, ro, rs)
    bo[opposite] = ro[opposite]
    bs[opposite] = rs[opposite]
    merge_part(opposite, bo, bs, acc, stats, out)
    lax.fori_loop(2, RING - 2, merge, 0)
    gone(q_copies + src_copies + far_copies)
    for stream in range(3):
        gone(spreading(stream) + sides(stream))


def copy_kernel(a, b, out_a, out_b, stage_a, stage_b, sem_in, sem_out):
    loads = [pltpu.make_async_copy(a, stage_a, sem_in.at[PARTS])]
    stores = [pltpu.make_async_copy(stage_a, out_a, sem_out.at[PARTS])]
    for i in range(PARTS):
        rows = pl.ds(i * (SEQ // PARTS), SEQ // PARTS)
        loads.append(pltpu.make_async_copy(b.at[rows], stage_b.at[rows], sem_in.at[i]))
        stores.append(pltpu.make_async_copy(stage_b.at[rows], out_b.at[rows], sem_out.at[i]))
    for copy in loads:
        copy.start()
    for load, store in zip(loads, stores):
        load.wait()
        store.start()
    for copy in stores:
        copy.wait()


def shards(
    prompt_q, prompt_kv, prefix_length, decode_q, decode_kv, fresh_kv, source_prompt, cache_length
):
    q = decode_q[0].reshape(SEQ, STEPS, HEADS, HD).transpose(0, 2, 1, 3)
    q = q.reshape(SEQ, KVH, ROWS, HD)
    fresh = fresh_kv[0].reshape(SEQ, 2, STEPS, KVH, HD).transpose(0, 1, 3, 2, 4)
    fresh = fresh.reshape(SEQ, 2, KVH * STEPS, HD)
    src = source_prompt[0, :, 0][None, :]
    vmem = pl.BlockSpec(memory_space=VMEM)
    smem = pl.BlockSpec(memory_space=pltpu.SMEM)
    anys = pl.BlockSpec(memory_space=pl.ANY)
    shape = jax.ShapeDtypeStruct
    sem = pltpu.SemaphoreType.DMA
    prompt_out, out = pl.pallas_call(
        kernel,
        out_shape=(
            shape((1, C, 2 * PER_KV * HD), BF16),
            shape((SEQ, KVH, ROWS, HD), BF16),
        ),
        in_specs=[smem, smem, anys, anys, anys, anys, anys, anys],
        out_specs=[vmem] * 2,
        scratch_shapes=[
            VMEM((2, KEYS, HD), BF16),
            VMEM((2, KEYS + 16, HD), BF16),
            VMEM((SLOTS, NZH, KEYS, HD), BF16),
            VMEM((SLOTS, NZH, KEYS + 16, HD), BF16),
            VMEM((SLOTS, NZH, KEYS, HD), BF16),
            VMEM((SLOTS, NZH, KEYS + 16, HD), BF16),
            VMEM((RING, SEQ, ROWS, HD), BF16),
            VMEM((RING, 1, SEQ), jnp.int32),
            pltpu.SMEM((RING, 1, SEQ), jnp.int32),
            VMEM((RING, SEQ, ROWS, HD), BF16),
            VMEM((RING, 8, 128), F32),
            VMEM((RING, SEQ, ROWS, HD), BF16),
            VMEM((RING, 8, 128), F32),
            VMEM((SEQ, KVH * ROWS, HD), F32),
            VMEM((KVH * ROWS, 128), F32),
            VMEM((1, C, 2 * PER_KV * HD), BF16),
            VMEM((SEQ, KVH, ROWS, HD), BF16),
            VMEM((SEQ, 2, LOC, KVH * HD), BF16),
            VMEM((SEQ, 2, KVH * STEPS, HD), BF16),
            sem((8,)),
            sem((4,)),
        ]
        + [sem((RING - 1,))] * 4
        + [sem((4,))] * 2
        + [sem((3, 2, 4))] * 2
        + [sem((3, 2, 4, 4))] * 2
        + [sem((3, 2, 4, 4))] * 2
        + [sem((RING,))] * 4,
        compiler_params=pltpu.CompilerParams(
            collective_id=0, has_side_effects=True, vmem_limit_bytes=58 * MIB
        ),
        name="attention",
    )(prefix_length, cache_length[0], prompt_q, prompt_kv, q, decode_kv[0], fresh, src)
    prompt_out, out = pl.pallas_call(
        copy_kernel,
        out_shape=(shape(prompt_out.shape, BF16), shape(out.shape, BF16)),
        in_specs=[anys] * 2,
        out_specs=[anys] * 2,
        scratch_shapes=[
            VMEM(prompt_out.shape, BF16),
            VMEM(out.shape, BF16),
            sem((PARTS + 1,)),
            sem((PARTS + 1,)),
        ],
        name="place",
    )(prompt_out, out)
    out = out.reshape(SEQ, HEADS, STEPS, HD).transpose(0, 2, 1, 3)
    return prompt_out, out.reshape(1, SEQ, STEPS, HEADS * HD)


def solution(mesh):
    return jax.shard_map(
        shards,
        mesh=mesh,
        in_specs=(
            P("role", None, "tp"),
            P("role", None, None, "tp"),
            P("role"),
            P("role", "tp", None, None),
            P("role", "tp", None, None, None),
            P("role", "tp", None, None, None),
            P("role", "tp", None),
            P("role", "tp"),
        ),
        out_specs=(P("role", None, "tp"), P("role", "tp", None, None)),
        check_vma=False,
    )
```
